256 devices in a mesh: ctx: 64 (over z, y_hi, x), head: 4 (over y_lo, core).
Axes of the slice: x: 4, y: 4 (y_hi: 2, y_lo: 2; y = y_hi * 2 + y_lo), z: 8, core: 2. Of those that a mesh axis runs over, the one named last changes fastest.
Arguments:
- tokens: bfloat16 [16384, 4096], P('ctx', 'head'), may hold values from -96 to 96
- w_query: bfloat16 [4096, 2048], P(None, 'head'), may hold values from -0.1875 to 0.1875
- key_matrix: bfloat16 [4096, 512], P(None, 'head'), may hold values from -0.09375 to 0.09375
- value_matrix: bfloat16 [4096, 512], P(None, 'head'), may hold values from -0.09375 to 0.09375
- w_output: bfloat16 [2048, 4096], P('head'), may hold values from -0.125 to 0.125
Outputs:
- mixed: bfloat16 [16384, 4096], P('ctx', 'head')
The draws below stay inside these ranges and needn't reach their ends.
All inputs are finite; a program needn't handle non-finite values.
Results may differ from the reference program's by a relative error of at most 0.013.
The reference program's roundings to bfloat16 on the way (of `query`, `keys`, `values`, `rounded` and `attended`) count: a program that leaves them out, or rounds other values in their place, can miss the bound.
Values may be sent and summed in bfloat16 or wider, within the bound.
No kernel may reach another device: no remote copies, remote signals or barrier semaphores. Data moves between devices by JAX's collectives and lax.ppermute only.
A program may use at most 64 MiB of HBM per device.

```python
import jax
import jax.numpy as jnp
from jax import lax

MODEL_WIDTH = 4096
QUERY_HEADS = 16
KEY_VALUE_HEADS = 4
HEAD_SIZE = 128
LENGTH = 16384


def draw_tokens(key, part):
    rows = LENGTH
    base = jnp.clip(jax.random.normal(jax.random.fold_in(key, 1), (rows, MODEL_WIDTH), jnp.float32), -6.0, 6.0)
    return base.astype(jnp.bfloat16)


def steps_of(own_key, shape, shards, low, top_value):
    factor_of = 1.0
    for axis_at, blocks in shards:
        draws = jax.random.uniform(jax.random.fold_in(jax.random.fold_in(own_key, 6), axis_at), (blocks,), jnp.float32, low / len(shards), top_value / len(shards))
        factor_of = factor_of * jnp.repeat(jnp.exp(draws), shape[axis_at] // blocks).reshape((-1,) + (1,) * (len(shape) - 1 - axis_at))
    return factor_of


def noise(own_key, dims, deviation, most, cuts=(), kind=jnp.bfloat16):
    entries = deviation * jax.random.normal(own_key, dims, jnp.float32)
    if cuts:
        entries = entries * steps_of(own_key, dims, cuts, -0.22, 0.18)
    return jnp.clip(entries, -most, most).astype(kind)


def setup_inputs(seed: int = 0) -> dict:
    arg_keys = jax.random.split(jax.random.key(seed), 6)
    tokens = draw_tokens(jax.random.fold_in(arg_keys[5], 71), 0)
    w_query = noise(arg_keys[1], (MODEL_WIDTH, QUERY_HEADS * HEAD_SIZE), (MODEL_WIDTH // 4) ** -0.5, 0.1875, ((1, 4),))
    key_matrix = noise(arg_keys[2], (MODEL_WIDTH, KEY_VALUE_HEADS * HEAD_SIZE), MODEL_WIDTH ** -0.5, 0.09375, ((1, 4),))
    value_matrix = noise(arg_keys[3], (MODEL_WIDTH, KEY_VALUE_HEADS * HEAD_SIZE), MODEL_WIDTH ** -0.5, 0.09375, ((1, 4),))
    w_output = noise(arg_keys[4], (QUERY_HEADS * HEAD_SIZE, MODEL_WIDTH), (QUERY_HEADS * HEAD_SIZE) ** -0.5, 0.125, ((0, 4),))
    return {"tokens": tokens, "w_query": w_query, "key_matrix": key_matrix, "value_matrix": value_matrix, "w_output": w_output}


neg_large = -1.0e30


def reference(tokens, w_query, key_matrix, value_matrix, w_output):
    query = jnp.dot(tokens, w_query, preferred_element_type=jnp.float32).astype(jnp.bfloat16)
    keys = jnp.dot(tokens, key_matrix, preferred_element_type=jnp.float32).astype(jnp.bfloat16)
    values = jnp.dot(tokens, value_matrix, preferred_element_type=jnp.float32).astype(jnp.bfloat16)
    query_group = QUERY_HEADS // KEY_VALUE_HEADS
    scale = HEAD_SIZE ** -0.5
    block = min(512, LENGTH)
    blocks = LENGTH // block
    positions = jnp.arange(LENGTH, dtype=jnp.int32)

    def head_cluster(index):
        key_head = lax.dynamic_slice_in_dim(keys, index * HEAD_SIZE, HEAD_SIZE, 1).astype(jnp.float32)
        value_head = lax.dynamic_slice_in_dim(values, index * HEAD_SIZE, HEAD_SIZE, 1).astype(jnp.float32)
        query_heads = lax.dynamic_slice_in_dim(query, index * query_group * HEAD_SIZE, query_group * HEAD_SIZE, 1).reshape(LENGTH, query_group, HEAD_SIZE)

        def query_block(block_index):
            first = block_index * block
            piece = lax.dynamic_slice_in_dim(query_heads, first, block, 0).astype(jnp.float32)
            scores = jnp.einsum("qgd,td->gqt", piece, key_head) * scale
            query_places = first + jnp.arange(block, dtype=jnp.int32)
            allowed = positions[None, :] <= query_places[:, None]
            top = jnp.max(jnp.where(allowed, scores, neg_large), axis=-1)
            weights = jnp.where(allowed, jnp.exp(scores - top[..., None]), 0.0)
            total = jnp.sum(weights, axis=-1)
            rounded = lax.optimization_barrier(weights.astype(jnp.bfloat16))
            summed = jnp.einsum("gqt,td->gqd", rounded.astype(jnp.float32), value_head)
            return (summed / total[..., None]).astype(jnp.bfloat16)

        output = lax.map(query_block, jnp.arange(blocks, dtype=jnp.int32))
        return output.transpose(0, 2, 1, 3).reshape(LENGTH, query_group * HEAD_SIZE)

    head_list = lax.map(head_cluster, jnp.arange(KEY_VALUE_HEADS, dtype=jnp.int32))
    attended = head_list.transpose(1, 0, 2).reshape(LENGTH, QUERY_HEADS * HEAD_SIZE)
    return jnp.dot(attended, w_output, preferred_element_type=jnp.float32).astype(jnp.bfloat16)
```

```python
import jax
import jax.numpy as jnp
from jax import lax
from jax.experimental import pallas as pl
from jax.experimental.pallas import tpu as pltpu
from jax.sharding import PartitionSpec as P

HEAD = 128
GROUP = 4
NZ, NY, NX = 8, 2, 4
ROWS = 256
STAT_ROWS = 16
NEG = -1e30
SCALE = HEAD**-0.5
LOG2E = 1.4426950408889634
C2 = SCALE * LOG2E
BF = jnp.bfloat16
F32 = jnp.float32
VMEM = pltpu.CompilerParams(vmem_limit_bytes=48 * 1024 * 1024)


def place(z, y, x):
    return (z % NZ) * (NY * NX) + (y % NY) * NX + x % NX


def shift(dz, dy, dx):
    return [
        (place(z, y, x), place(z + dz, y + dy, x + dx))
        for z in range(NZ)
        for y in range(NY)
        for x in range(NX)
    ]


def swap(bit):
    return [(h, h ^ bit) for h in range(4)]


def partial_products(blocks, first, second, weights, sums, out_type):
    rows, depth = first.shape
    count = len(weights)
    started = sums is not None

    def body(blocks_ref, first_ref, second_ref, *refs):
        w_refs = refs[:count]
        s_refs = refs[count : 2 * count] if started else ()
        o_refs = refs[-2 * count : -count]
        a_refs = refs[-count:]
        step = pl.program_id(0)

        @pl.when(step == 0)
        def _():
            for n in range(count):
                t = jnp.dot(first_ref[...], w_refs[n][...], preferred_element_type=F32)
                a_refs[n][...] = t + s_refs[n][...] if started else t

        @pl.when(step == 1)
        def _():
            for n in range(count):
                t = jnp.dot(second_ref[...], w_refs[n][...], preferred_element_type=F32)
                o_refs[n][...] = (a_refs[n][...] + t).astype(out_type)

    whole = lambda shape: pl.BlockSpec(shape, lambda i, b: (0, 0))
    in_specs = [whole(first.shape), whole(second.shape)]
    in_specs += [pl.BlockSpec((depth, w.shape[1]), lambda i, b: (b[i], 0)) for w in weights]
    operands = [first, second, *weights]
    if started:
        in_specs += [whole(s.shape) for s in sums]
        operands += list(sums)
    shapes = [(rows, w.shape[1]) for w in weights]
    return pl.pallas_call(
        body,
        grid_spec=pltpu.PrefetchScalarGridSpec(
            num_scalar_prefetch=1,
            grid=(2,),
            in_specs=in_specs,
            out_specs=[whole(s) for s in shapes],
            scratch_shapes=[pltpu.VMEM(s, F32) for s in shapes],
        ),
        out_shape=[jax.ShapeDtypeStruct(s, out_type) for s in shapes],
        compiler_params=VMEM,
        cost_estimate=pl.CostEstimate(
            flops=2 * 10**9, bytes_accessed=8 * 10**6, transcendentals=0
        ),
    )(blocks, *operands)


def attention_body(place_ref, *refs):
    q_refs = refs[:4]
    own_ref, other_ref = refs[4:6]
    up_refs = refs[6:10]
    down_refs = refs[10:13]
    out_refs = refs[13:17]
    m_ref, l_ref, acc_ref = refs[17:20]
    z, y, x = place_ref[0], place_ref[1], place_ref[2]

    def tile(d, h, keys, values, mask, fresh):
        slot = d * GROUP + h
        q = q_refs[d][:, h * HEAD : (h + 1) * HEAD]
        s = lax.dot_general(q, keys, (((1,), (1,)), ((), ())), preferred_element_type=F32)
        if mask is not None:
            s = jnp.where(mask, s, NEG)
        top = jnp.max(s, axis=1, keepdims=True)
        if fresh:
            m_new = jnp.broadcast_to(top, (ROWS, HEAD))
        else:
            m_old = m_ref[slot]
            m_new = jnp.maximum(m_old, top)
        width = s.shape[1] // HEAD
        parts = []
        total = None
        for n in range(width):
            p = jnp.exp2((s[:, n * HEAD : (n + 1) * HEAD] - m_new) * C2)
            if mask is not None:
                p = jnp.where(mask[:, n * HEAD : (n + 1) * HEAD], p, 0.0)
            total = p if total is None else total + p
            parts.append(p.astype(BF))
        pv = jnp.dot(jnp.concatenate(parts, axis=1), values, preferred_element_type=F32)
        m_ref[slot] = m_new
        if fresh:
            l_ref[slot] = total
            acc_ref[slot] = pv
        else:
            factor = jnp.exp2((m_old - m_new) * C2)
            l_ref[slot] = l_ref[slot] * factor + total
            acc_ref[slot] = acc_ref[slot] * factor + pv

    row = lax.broadcasted_iota(jnp.int32, (ROWS, ROWS), 0)
    col = lax.broadcasted_iota(jnp.int32, (ROWS, ROWS), 1)
    for d in range(NX):
        xq = lax.rem(x + d, NX)
        ahead = (xq - x) * ROWS
        mask = col <= row + ahead
        for h in range(GROUP):
            tile(d, h, own_ref[:, :HEAD], own_ref[:, HEAD:], mask, True)

    def block(ref):
        for d in range(NX):
            for h in range(GROUP):
                tile(d, h, ref[:, :HEAD], ref[:, HEAD:], None, False)

    @pl.when(y == 1)
    def _():
        block(other_ref)

    for s in range(1, 5):

        @pl.when(z >= s)
        def _():
            block(up_refs[s - 1])

    for s in range(1, 4):

        @pl.when(z >= NZ - s)
        def _():
            block(down_refs[s - 1])

    lane = lax.broadcasted_iota(jnp.int32, (ROWS, HEAD), 1)
    for d in range(NX):
        stats = jnp.zeros((ROWS, HEAD), F32)
        for h in range(GROUP):
            slot = d * GROUP + h
            total = jnp.sum(l_ref[slot], axis=1, keepdims=True)
            scale = jnp.where(total > 0.0, 1.0 / total, 0.0)
            out_refs[d][:ROWS, h * HEAD : (h + 1) * HEAD] = (acc_ref[slot] * scale).astype(BF)
            stats = jnp.where(lane == h, m_ref[slot], stats)
            stats = jnp.where(lane == GROUP + h, total, stats)
        flat = stats.T[: 2 * GROUP]
        hi = flat.astype(BF)
        rest = flat - hi.astype(F32)
        mid = rest.astype(BF)
        low = (rest - mid.astype(F32)).astype(BF)
        left = jnp.concatenate([hi.astype(F32), mid.astype(F32)], axis=0)
        right = jnp.concatenate([low.astype(F32), jnp.zeros_like(flat)], axis=0)
        out_refs[d][ROWS:, :] = jnp.concatenate([left, right], axis=1).astype(BF)


def attention(where, queries, own, other, ups, downs):
    operands = [*queries, own, other, *ups, *downs]
    whole = lambda a: pl.BlockSpec(a.shape, lambda i, p: (0, 0))
    out = jax.ShapeDtypeStruct((ROWS + STAT_ROWS, GROUP * HEAD), BF)
    return pl.pallas_call(
        attention_body,
        grid_spec=pltpu.PrefetchScalarGridSpec(
            num_scalar_prefetch=1,
            grid=(1,),
            in_specs=[whole(a) for a in operands],
            out_specs=[whole(out)] * NX,
            scratch_shapes=[
                pltpu.VMEM((NX * GROUP, ROWS, HEAD), F32),
                pltpu.VMEM((NX * GROUP, ROWS, HEAD), F32),
                pltpu.VMEM((NX * GROUP, ROWS, HEAD), F32),
            ],
        ),
        out_shape=[out] * NX,
        compiler_params=VMEM,
        cost_estimate=pl.CostEstimate(
            flops=2 * 10**10, bytes_accessed=8 * 10**6, transcendentals=2 * 10**7
        ),
    )(where, *operands)


def combine_body(*refs):
    part_refs, out_ref = refs[:NX], refs[NX]
    stats = []
    for ref in part_refs:
        packed = ref[ROWS:, :].astype(F32)
        left, right = packed[:, :ROWS], packed[:, ROWS:]
        flat = left[: 2 * GROUP] + left[2 * GROUP :] + right[: 2 * GROUP]
        tall = jnp.concatenate([flat] * (HEAD // (2 * GROUP)), axis=0)
        stats.append(tall.T)
    for h in range(GROUP):
        tops = [s[:, h : h + 1] for s in stats]
        best = tops[0]
        for t in tops[1:]:
            best = jnp.maximum(best, t)
        weights = [
            s[:, GROUP + h : GROUP + h + 1] * jnp.exp2((t - best) * C2)
            for s, t in zip(stats, tops)
        ]
        whole = weights[0]
        for w in weights[1:]:
            whole = whole + w
        inverse = 1.0 / whole
        cols = slice(h * HEAD, (h + 1) * HEAD)
        mixed = None
        for w, ref in zip(weights, part_refs):
            term = ref[:ROWS, cols].astype(F32) * (w * inverse)
            mixed = term if mixed is None else mixed + term
        out_ref[:, cols] = mixed.astype(BF)


def combine(parts):
    return pl.pallas_call(
        combine_body,
        out_shape=jax.ShapeDtypeStruct((ROWS, GROUP * HEAD), BF),
        compiler_params=VMEM,
    )(*parts)


def local(tokens, w_query, key_matrix, value_matrix, w_output):
    c = lax.axis_index("ctx").astype(jnp.int32)
    h = lax.axis_index("head").astype(jnp.int32)
    z, y, x = c // (NY * NX), (c // NX) % NY, c % NX
    where = jnp.stack([z, y, x])
    near = jnp.stack([h, h ^ 1])
    far = jnp.stack([h ^ 2, h ^ 3])

    t_chip = lax.ppermute(tokens, "head", swap(2))
    t_core = lax.ppermute(tokens, "head", swap(1))
    sums = partial_products(near, tokens, t_core, (w_query, key_matrix, value_matrix), None, F32)
    t_far = lax.ppermute(t_chip, "head", swap(1))
    keys, values = partial_products(
        far, t_chip, t_far, (key_matrix, value_matrix), sums[1:], BF
    )
    own = jnp.concatenate([keys, values], axis=1)
    other = lax.ppermute(own, "ctx", shift(0, 1, 0))
    (query,) = partial_products(far, t_chip, t_far, (w_query,), sums[:1], BF)
    queries = [query] + [lax.ppermute(query, "ctx", shift(0, 0, -d)) for d in range(1, NX)]
    level = jnp.concatenate([own, other], axis=0)
    w_output, level = lax.optimization_barrier((w_output, level))
    ups, downs = [], []
    held_up = held_down = level
    for s in range(1, 5):
        held_up = lax.ppermute(held_up, "ctx", shift(1, 0, 0))
        ups.append(held_up)
        if s < 4:
            held_down = lax.ppermute(held_down, "ctx", shift(-1, 0, 0))
            downs.append(held_down)
    turned = lax.all_to_all(w_output, "head", 1, 0, tiled=True)
    parts = attention(where, queries, own, other, ups, downs)
    parts = [parts[0]] + [
        lax.ppermute(parts[d], "ctx", shift(0, 0, d)) for d in range(1, NX)
    ]
    attended = combine(parts)
    a_chip = lax.ppermute(attended, "head", swap(2))
    a_core = lax.ppermute(attended, "head", swap(1))
    a_far = lax.ppermute(a_chip, "head", swap(1))
    (half,) = partial_products(near, attended, a_core, (turned,), None, F32)
    (mixed,) = partial_products(far, a_chip, a_far, (turned,), (half,), BF)
    return mixed


def solution(mesh):
    return jax.shard_map(
        local,
        mesh=mesh,
        in_specs=(
            P("ctx", "head"),
            P(None, "head"),
            P(None, "head"),
            P(None, "head"),
            P("head", None),
        ),
        out_specs=P("ctx", "head"),
        check_vma=False,
    )
```

```python
import functools

import jax
import jax.numpy as jnp
from jax import lax
from jax.experimental import pallas as pl
from jax.experimental.pallas import tpu as pltpu
from jax.sharding import PartitionSpec as P

HEAD = 128
GROUP = 4
NZ, NY, NX = 8, 2, 4
ROWS = 256
WIDE = GROUP * ROWS
PAIR = 2 * WIDE
STAT_ROWS = 32
OUT_ROWS = GROUP * HEAD + STAT_ROWS
NEG = -1e30
C2 = HEAD**-0.5 * 1.4426950408889634
BF = jnp.bfloat16
F32 = jnp.float32
MIB = 1024 * 1024
SMALL = pltpu.CompilerParams(vmem_limit_bytes=16 * MIB)
LARGE = pltpu.CompilerParams(vmem_limit_bytes=24 * MIB)
IN_VMEM = pl.BlockSpec(memory_space=pltpu.VMEM)
IN_SMEM = pl.BlockSpec(memory_space=pltpu.SMEM)
IN_HBM = pl.BlockSpec(memory_space=pltpu.HBM)
ANYWHERE = pl.BlockSpec(memory_space=pl.ANY)


def place(z, y, x):
    return (z % NZ) * (NY * NX) + (y % NY) * NX + x % NX


def shift(dz, dy, dx):
    return [
        (place(z, y, x), place(z + dz, y + dy, x + dx))
        for z in range(NZ)
        for y in range(NY)
        for x in range(NX)
    ]


def swap(bit):
    return [(h, h ^ bit) for h in range(4)]


def cost(us):
    return pl.CostEstimate(
        flops=int(us * 10**9), bytes_accessed=int(us * 3 * 10**6), transcendentals=0
    )


def project_near(near, far, first, second, weights, after, us):
    depth = first.shape[1]
    count = len(weights)

    def rows(blocks_ref, step):
        return pl.ds(pl.multiple_of(blocks_ref[step] * depth, depth), depth)

    def body(near_ref, far_ref, first_ref, second_ref, *refs):
        w_refs, refs = refs[:count], refs[count + len(after) :]
        s_refs, f_refs, done_ref = refs[:count], refs[count : 2 * count], refs[-1]
        done_ref[...] = jnp.zeros(done_ref.shape, F32)
        for n in range(count):
            s_refs[n][...] = jnp.dot(
                first_ref[...], w_refs[n][rows(near_ref, 0), :], preferred_element_type=F32
            ) + jnp.dot(
                second_ref[...], w_refs[n][rows(near_ref, 1), :], preferred_element_type=F32
            )
            for step in range(2):
                f_refs[n][step] = w_refs[n][rows(far_ref, step), :]

    widths = [w.shape[1] for w in weights]
    out = pl.pallas_call(
        body,
        in_specs=[IN_SMEM] * 2 + [IN_VMEM] * (2 + count) + [ANYWHERE] * len(after),
        out_specs=[IN_VMEM] * (2 * count + 1),
        out_shape=[jax.ShapeDtypeStruct((first.shape[0], n), F32) for n in widths]
        + [jax.ShapeDtypeStruct((2, depth, n), BF) for n in widths]
        + [jax.ShapeDtypeStruct((8, HEAD), F32)],
        compiler_params=SMALL,
        cost_estimate=cost(us),
    )(near, far, first, second, *weights, *after)
    return out[:count], out[count : 2 * count], out[-1]


def project_far(first, second, weights, sums, after, finish, shape, us):
    count = len(weights)

    def body(first_ref, second_ref, *refs):
        w_refs, s_refs = refs[:count], refs[count : 2 * count]
        totals = []
        for n in range(count):
            total = s_refs[n][...] + jnp.dot(
                first_ref[...], w_refs[n][0], preferred_element_type=F32
            )
            totals.append(
                total + jnp.dot(second_ref[...], w_refs[n][1], preferred_element_type=F32)
            )
        finish(totals, refs[-1])

    return pl.pallas_call(
        body,
        in_specs=[IN_VMEM] * (2 + 2 * count) + [ANYWHERE] * len(after),
        out_specs=IN_VMEM,
        out_shape=jax.ShapeDtypeStruct(shape, BF),
        compiler_params=SMALL,
        cost_estimate=cost(us),
    )(first, second, *weights, *sums, *after)


def pair_up(own, other, after):
    def body(own_ref, other_ref, *refs):
        refs[-1][0] = own_ref[...]
        refs[-1][1] = other_ref[...]

    return pl.pallas_call(
        body,
        in_specs=[IN_VMEM] * 2 + [ANYWHERE] * len(after),
        out_specs=IN_VMEM,
        out_shape=jax.ShapeDtypeStruct((2,) + own.shape, own.dtype),
        compiler_params=SMALL,
        cost_estimate=cost(1),
    )(own, other, *after)


def columns_apart(w, width):
    count = w.shape[1] // width

    def body(w_ref, o_ref, sem):
        copies = [
            pltpu.make_async_copy(
                w_ref.at[:, pl.ds(n * width, width)], o_ref.at[n], sem.at[n]
            )
            for n in range(count)
        ]
        for c in copies:
            c.start()
        for c in copies:
            c.wait()

    return pl.pallas_call(
        body,
        in_specs=[IN_HBM],
        out_specs=IN_HBM,
        out_shape=jax.ShapeDtypeStruct((count, w.shape[0], width), w.dtype),
        scratch_shapes=[pltpu.SemaphoreType.DMA((count,))],
        compiler_params=SMALL,
        cost_estimate=cost(3),
    )(w)


def store_keys_values(totals, out):
    keys, values = totals
    turned = values.T.astype(BF)
    out[:ROWS] = keys.astype(BF)
    out[ROWS : ROWS + HEAD] = turned[:, :HEAD]
    out[ROWS + HEAD :] = turned[:, HEAD:]


def store_turned(totals, out):
    out[...] = totals[0].T.astype(BF)


def products(blocks, lefts, pieces, sums, out_type, us):
    extra = 0 if sums is None else 1
    count = len(lefts)

    def body(blocks_ref, pieces_ref, *refs):
        held, sem = refs[-2:]
        copies = [
            pltpu.make_async_copy(pieces_ref.at[blocks_ref[n]], held.at[n], sem.at[n])
            for n in range(count)
        ]
        for c in copies:
            c.start()
        total = refs[count][...] if extra else None
        for n in range(count):
            copies[n].wait()
            term = jnp.dot(refs[n][...], held[n], preferred_element_type=F32)
            total = term if total is None else total + term
        refs[-3][...] = total.astype(out_type)

    operands = list(lefts) + ([] if sums is None else [sums])
    return pl.pallas_call(
        body,
        in_specs=[IN_SMEM, IN_HBM] + [IN_VMEM] * len(operands),
        out_specs=IN_VMEM,
        out_shape=jax.ShapeDtypeStruct((lefts[0].shape[0], pieces.shape[2]), out_type),
        scratch_shapes=[
            pltpu.VMEM((count,) + pieces.shape[1:], BF),
            pltpu.SemaphoreType.DMA((count,)),
        ],
        compiler_params=SMALL,
        cost_estimate=cost(us),
    )(blocks, pieces, *operands)


def keys_of(ref):
    if len(ref.shape) == 2:
        return ref[:ROWS, :]
    return jnp.concatenate([ref[0, :ROWS, :], ref[1, :ROWS, :]], axis=0)


def values_of(ref):
    if len(ref.shape) == 2:
        return jnp.concatenate([ref[ROWS : ROWS + HEAD, :], ref[ROWS + HEAD :, :]], axis=1)
    return jnp.concatenate(
        [
            ref[0, ROWS : ROWS + HEAD, :],
            ref[0, ROWS + HEAD :, :],
            ref[1, ROWS : ROWS + HEAD, :],
            ref[1, ROWS + HEAD :, :],
        ],
        axis=1,
    )


def queries_of(q_refs, group):
    return jnp.concatenate(
        [q_refs[d][h * HEAD : (h + 1) * HEAD, :] for d in group for h in range(GROUP)], axis=1
    )


def fold(s):
    return jnp.sum(s.reshape(s.shape[0] // 8, 8, s.shape[1]), axis=0)


def attend_body(kinds, first, pairs, where_ref, *refs):
    last = pairs is not None
    pairs = list(range(NX // 2)) if pairs is None else pairs
    q_refs, refs = refs[:NX], refs[NX:]
    kv_refs, refs = refs[: len(kinds)], refs[len(kinds) :]
    if not first:
        old, refs = refs[:3], refs[3:]
    if last:
        out_refs, refs = refs[: 2 * len(pairs)], refs[2 * len(pairs) :]
    m_ref, l_ref, acc_ref = refs
    z, y, x = where_ref[0], where_ref[1], where_ref[2]
    if first:
        m_ref[...] = jnp.full(m_ref.shape, NEG, F32)
        l_ref[...] = jnp.zeros(l_ref.shape, F32)
        acc_ref[...] = jnp.zeros(acc_ref.shape, F32)
    else:
        for pair in pairs:
            cols = slice(pair * PAIR, (pair + 1) * PAIR)
            for new_ref, old_ref in zip((m_ref, l_ref, acc_ref), old):
                new_ref[:, cols] = old_ref[:, cols]

    def diagonal(d, ref):
        ahead = (lax.rem(x + d, NX) - x) * ROWS
        cols = slice(d * WIDE, (d + 1) * WIDE)

        @pl.when(ahead >= 0)
        def _():
            q = queries_of(q_refs, [d])
            s = jnp.dot(keys_of(ref), q, preferred_element_type=F32)
            key = lax.broadcasted_iota(jnp.int32, s.shape, 0)
            query = lax.broadcasted_iota(jnp.int32, s.shape, 1) % ROWS
            seen = key <= query + ahead
            s = jnp.where(seen, s, NEG)
            top = jnp.max(s, axis=0, keepdims=True)
            p = jnp.where(seen, jnp.exp2((s - top) * C2), 0.0)
            m_ref[:, cols] = top
            l_ref[:, cols] = fold(p)
            acc_ref[:, cols] = jnp.dot(values_of(ref), p.astype(BF), preferred_element_type=F32)

    def whole(ref):
        keys, values = keys_of(ref), values_of(ref)
        for pair in pairs:
            cols = slice(pair * PAIR, (pair + 1) * PAIR)
            q = queries_of(q_refs, [2 * pair, 2 * pair + 1])
            s = jnp.dot(keys, q, preferred_element_type=F32)
            m_old = m_ref[:, cols]
            m_new = jnp.maximum(m_old, jnp.max(s, axis=0, keepdims=True))
            p = jnp.exp2((s - m_new) * C2)
            total = fold(p)
            add = jnp.dot(values, p.astype(BF), preferred_element_type=F32)
            factor = jnp.exp2((m_old - m_new) * C2)
            m_ref[:, cols] = m_new
            l_ref[:, cols] = l_ref[:, cols] * factor + total
            acc_ref[:, cols] = acc_ref[:, cols] * factor + add

    for kind, ref in zip(kinds, kv_refs):
        name, steps = kind
        if name == "own":
            for d in range(NX):
                diagonal(d, ref)
        elif name == "other":
            pl.when(y == 1)(functools.partial(whole, ref))
        elif name == "up":
            pl.when(z >= steps)(functools.partial(whole, ref))
        else:
            pl.when(z >= NZ - steps)(functools.partial(whole, ref))

    if last:
        for place_at, d in enumerate([d for pair in pairs for d in (2 * pair, 2 * pair + 1)]):
            out_ref = out_refs[place_at]
            tops, totals = [], []
            for h in range(GROUP):
                cols = slice((d * GROUP + h) * ROWS, (d * GROUP + h + 1) * ROWS)
                total = jnp.sum(l_ref[:, cols], axis=0, keepdims=True)
                scale = jnp.where(total > 0.0, 1.0 / total, 0.0)
                out_ref[h * HEAD : (h + 1) * HEAD, :] = (acc_ref[:, cols] * scale).astype(BF)
                tops.append(m_ref[:, cols])
                totals.append(total)
            flat = jnp.concatenate(tops + totals, axis=0)
            hi = flat.astype(BF).astype(F32)
            mid = (flat - hi).astype(BF).astype(F32)
            low = flat - hi - mid
            packed = jnp.concatenate([hi, mid, low, jnp.zeros_like(flat)], axis=0)
            out_ref[GROUP * HEAD :, :] = packed.astype(BF)


STATE = [(1, NX * WIDE), (8, NX * WIDE), (HEAD, NX * WIDE)]


def attend(where, queries, blocks, state, pairs, us):
    kinds = [k for k, _ in blocks]
    first = state is None
    operands = [*queries, *[a for _, a in blocks]] + ([] if first else list(state))
    if pairs is not None:
        shapes = [jax.ShapeDtypeStruct((OUT_ROWS, ROWS), BF)] * (2 * len(pairs))
        scratch = [pltpu.VMEM(s, F32) for s in STATE]
    else:
        shapes = [jax.ShapeDtypeStruct(s, F32) for s in STATE]
        scratch = []
    return pl.pallas_call(
        functools.partial(attend_body, kinds, first, pairs),
        in_specs=[IN_SMEM] + [IN_VMEM] * len(operands),
        out_specs=[IN_VMEM] * len(shapes),
        out_shape=shapes,
        scratch_shapes=scratch,
        compiler_params=LARGE,
        cost_estimate=cost(us),
    )(where, *operands)


def combine_body(*refs):
    part_refs, out_ref = refs[:NX], refs[NX]
    tops, totals = [], []
    for ref in part_refs:
        packed = ref[GROUP * HEAD :, :].astype(F32)
        flat = packed[:8] + packed[8:16] + packed[16:24]
        tops.append(flat[:GROUP])
        totals.append(flat[GROUP:])
    best = functools.reduce(jnp.maximum, tops)
    weights = [t * jnp.exp2((m - best) * C2) for m, t in zip(tops, totals)]
    inverse = 1.0 / functools.reduce(jnp.add, weights)
    weights = [w * inverse for w in weights]
    for h in range(GROUP):
        rows = slice(h * HEAD, (h + 1) * HEAD)
        mixed = functools.reduce(
            jnp.add,
            [ref[rows, :].astype(F32) * w[h : h + 1] for ref, w in zip(part_refs, weights)],
        )
        out_ref[:, rows] = mixed.T.astype(BF)


def combine(parts):
    return pl.pallas_call(
        combine_body,
        in_specs=[IN_VMEM] * NX,
        out_specs=IN_VMEM,
        out_shape=jax.ShapeDtypeStruct((ROWS, GROUP * HEAD), BF),
        compiler_params=SMALL,
        cost_estimate=cost(1),
    )(*parts)


def local(tokens, w_query, key_matrix, value_matrix, w_output):
    c = lax.axis_index("ctx").astype(jnp.int32)
    h = lax.axis_index("head").astype(jnp.int32)
    where = jnp.stack([c // (NY * NX), (c // NX) % NY, c % NX])
    near = jnp.stack([h, h ^ 1])
    far = jnp.stack([h ^ 2, h ^ 3])
    width = tokens.shape[1]
    t_core = lax.ppermute(tokens, "head", swap(1))
    t_chip = lax.ppermute(tokens, "head", swap(2))
    slices = columns_apart(w_output, width)
    sums, rest, done = project_near(
        near, far, tokens, t_core, (w_query, key_matrix, value_matrix), [slices], 12
    )
    t_chip, done = lax.optimization_barrier((t_chip, done))
    t_far = lax.ppermute(t_chip, "head", swap(1))
    query = project_far(
        t_chip, t_far, rest[:1], sums[:1], [], store_turned, (GROUP * HEAD, ROWS), 2
    )
    own = project_far(
        t_chip, t_far, rest[1:], sums[1:], [query], store_keys_values, (2 * ROWS, HEAD), 2
    )
    other = lax.ppermute(own, "ctx", shift(0, 1, 0))
    queries = [query] + [lax.ppermute(query, "ctx", shift(0, 0, -d)) for d in range(1, NX)]
    slices, _ = lax.optimization_barrier((slices, other))
    pieces = lax.all_to_all(slices, "head", 0, 0, tiled=True)
    level = pair_up(own, other, queries)

    up = down = level
    state = None
    blocks = [(("own", 0), own), (("other", 0), other)]
    for s in range(1, 5):
        up = lax.ppermute(up, "ctx", shift(1, 0, 0))
        if s < 4:
            down = lax.ppermute(down, "ctx", shift(-1, 0, 0))
        if s > 1:
            state = attend(where, queries, blocks, state, None, 6)
            up, down, state = lax.optimization_barrier((up, down, state))
            blocks = [(("up", s - 1), last_up), (("down", s - 1), last_down)]
        last_up, last_down = up, down
    blocks += [(("up", 4), up)]
    parts = [None] * NX
    parts[2], parts[3] = attend(where, queries, blocks, state, [1], 6)
    sent = [None] * NX
    for d in (2, 3):
        sent[d] = lax.ppermute(parts[d], "ctx", shift(0, 0, d))
    parts[0], parts[1] = attend(where, queries, blocks, state, [0], 6)
    sent[0] = parts[0]
    sent[1] = lax.ppermute(parts[1], "ctx", shift(0, 0, 1))
    attended = combine(sent)
    a_chip = lax.ppermute(attended, "head", swap(2))
    a_core = lax.ppermute(attended, "head", swap(1))
    total = products(near, [attended, a_core], pieces, None, F32, 3)
    total, a_chip = lax.optimization_barrier((total, a_chip))
    a_far = lax.ppermute(a_chip, "head", swap(1))
    total = products(far[:1], [a_chip], pieces, total, F32, 2)
    return products(far[1:], [a_far], pieces, total, BF, 2)


def solution(mesh):
    return jax.shard_map(
        local,
        mesh=mesh,
        in_specs=(
            P("ctx", "head"),
            P(None, "head"),
            P(None, "head"),
            P(None, "head"),
            P("head", None),
        ),
        out_specs=P("ctx", "head"),
        check_vma=False,
    )
```

```python
import functools

import jax
import jax.numpy as jnp
from jax import lax
from jax.experimental import pallas as pl
from jax.experimental.pallas import tpu as pltpu
from jax.sharding import PartitionSpec as P

HEAD = 128
GROUP = 4
NZ, NY, NX = 8, 2, 4
ROWS = 256
WIDE = GROUP * ROWS
PAIR = 2 * WIDE
STAT_ROWS = 32
OUT_ROWS = GROUP * HEAD + STAT_ROWS
NEG = -1e30
C2 = HEAD**-0.5 * 1.4426950408889634
BF = jnp.bfloat16
F32 = jnp.float32
MIB = 1024 * 1024
SMALL = pltpu.CompilerParams(vmem_limit_bytes=16 * MIB)
LARGE = pltpu.CompilerParams(vmem_limit_bytes=40 * MIB)
IN_VMEM = pl.BlockSpec(memory_space=pltpu.VMEM)
IN_SMEM = pl.BlockSpec(memory_space=pltpu.SMEM)
IN_HBM = pl.BlockSpec(memory_space=pltpu.HBM)
ANYWHERE = pl.BlockSpec(memory_space=pl.ANY)


def place(z, y, x):
    return (z % NZ) * (NY * NX) + (y % NY) * NX + x % NX


def shift(dz, dy, dx):
    return [
        (place(z, y, x), place(z + dz, y + dy, x + dx))
        for z in range(NZ)
        for y in range(NY)
        for x in range(NX)
    ]


def swap(bit):
    return [(h, h ^ bit) for h in range(4)]


def cost(us):
    return pl.CostEstimate(
        flops=int(us * 10**9), bytes_accessed=int(us * 3 * 10**6), transcendentals=0
    )


def project_near(near, far, first, second, weights, after, us):
    depth = first.shape[1]
    count = len(weights)

    def rows(blocks_ref, step):
        return pl.ds(pl.multiple_of(blocks_ref[step] * depth, depth), depth)

    def body(near_ref, far_ref, first_ref, second_ref, *refs):
        w_refs, refs = refs[:count], refs[count + len(after) :]
        s_refs, f_refs, done_ref = refs[:count], refs[count : 2 * count], refs[-1]
        done_ref[...] = jnp.zeros(done_ref.shape, F32)
        for n in range(count):
            s_refs[n][...] = jnp.dot(
                first_ref[...], w_refs[n][rows(near_ref, 0), :], preferred_element_type=F32
            ) + jnp.dot(
                second_ref[...], w_refs[n][rows(near_ref, 1), :], preferred_element_type=F32
            )
            for step in range(2):
                f_refs[n][step] = w_refs[n][rows(far_ref, step), :]

    widths = [w.shape[1] for w in weights]
    out = pl.pallas_call(
        body,
        in_specs=[IN_SMEM] * 2 + [IN_VMEM] * (2 + count) + [ANYWHERE] * len(after),
        out_specs=[IN_VMEM] * (2 * count + 1),
        out_shape=[jax.ShapeDtypeStruct((first.shape[0], n), F32) for n in widths]
        + [jax.ShapeDtypeStruct((2, depth, n), BF) for n in widths]
        + [jax.ShapeDtypeStruct((8, HEAD), F32)],
        compiler_params=SMALL,
        cost_estimate=cost(us),
    )(near, far, first, second, *weights, *after)
    return out[:count], out[count : 2 * count], out[-1]


def project_far(first, second, weights, sums, after, finish, shape, us):
    count = len(weights)

    def body(first_ref, second_ref, *refs):
        w_refs, s_refs = refs[:count], refs[count : 2 * count]
        totals = []
        for n in range(count):
            total = s_refs[n][...] + jnp.dot(
                first_ref[...], w_refs[n][0], preferred_element_type=F32
            )
            totals.append(
                total + jnp.dot(second_ref[...], w_refs[n][1], preferred_element_type=F32)
            )
        finish(totals, refs[-1])

    return pl.pallas_call(
        body,
        in_specs=[IN_VMEM] * (2 + 2 * count) + [ANYWHERE] * len(after),
        out_specs=IN_VMEM,
        out_shape=jax.ShapeDtypeStruct(shape, BF),
        compiler_params=SMALL,
        cost_estimate=cost(us),
    )(first, second, *weights, *sums, *after)


def pair_up(own, other, after):
    def body(own_ref, other_ref, *refs):
        refs[-1][0] = own_ref[...]
        refs[-1][1] = other_ref[...]

    return pl.pallas_call(
        body,
        in_specs=[IN_VMEM] * 2 + [ANYWHERE] * len(after),
        out_specs=IN_VMEM,
        out_shape=jax.ShapeDtypeStruct((2,) + own.shape, own.dtype),
        compiler_params=SMALL,
        cost_estimate=cost(1),
    )(own, other, *after)


def columns_apart(w, width):
    count = w.shape[1] // width

    def body(w_ref, o_ref, sem):
        copies = [
            pltpu.make_async_copy(
                w_ref.at[:, pl.ds(n * width, width)], o_ref.at[n], sem.at[n]
            )
            for n in range(count)
        ]
        for c in copies:
            c.start()
        for c in copies:
            c.wait()

    return pl.pallas_call(
        body,
        in_specs=[IN_HBM],
        out_specs=IN_HBM,
        out_shape=jax.ShapeDtypeStruct((count, w.shape[0], width), w.dtype),
        scratch_shapes=[pltpu.SemaphoreType.DMA((count,))],
        compiler_params=SMALL,
        cost_estimate=cost(3),
    )(w)


def store_keys_values(totals, out):
    keys, values = totals
    turned = values.T.astype(BF)
    out[:ROWS] = keys.astype(BF)
    out[ROWS : ROWS + HEAD] = turned[:, :HEAD]
    out[ROWS + HEAD :] = turned[:, HEAD:]


def store_turned(totals, out):
    out[...] = totals[0].T.astype(BF)


def products_near(near, far, lefts, pieces, us):
    count = len(lefts)

    def body(near_ref, far_ref, pieces_ref, *refs):
        o_ref, rest_refs = refs[count], refs[count + 1 : count + 3]
        held, sem = refs[-2:]
        copies = [
            pltpu.make_async_copy(pieces_ref.at[near_ref[n]], held.at[n], sem.at[n])
            for n in range(count)
        ]
        copies += [
            pltpu.make_async_copy(pieces_ref.at[far_ref[n]], rest_refs[n], sem.at[count + n])
            for n in range(2)
        ]
        for c in copies:
            c.start()
        total = None
        for n in range(count):
            copies[n].wait()
            term = jnp.dot(refs[n][...], held[n], preferred_element_type=F32)
            total = term if total is None else total + term
        o_ref[...] = total
        for c in copies[count:]:
            c.wait()

    piece = jax.ShapeDtypeStruct(pieces.shape[1:], BF)
    total, *rest = pl.pallas_call(
        body,
        in_specs=[IN_SMEM] * 2 + [IN_HBM] + [IN_VMEM] * count,
        out_specs=[IN_VMEM] * 3,
        out_shape=[jax.ShapeDtypeStruct((lefts[0].shape[0], pieces.shape[2]), F32), piece, piece],
        scratch_shapes=[
            pltpu.VMEM((count,) + pieces.shape[1:], BF),
            pltpu.SemaphoreType.DMA((count + 2,)),
        ],
        compiler_params=SMALL,
        cost_estimate=cost(us),
    )(near, far, pieces, *lefts)
    return total, rest


def product(left, piece, total, out_type, us):
    def body(left_ref, piece_ref, total_ref, o_ref):
        term = jnp.dot(left_ref[...], piece_ref[...], preferred_element_type=F32)
        o_ref[...] = (total_ref[...] + term).astype(out_type)

    return pl.pallas_call(
        body,
        in_specs=[IN_VMEM] * 3,
        out_specs=IN_VMEM,
        out_shape=jax.ShapeDtypeStruct(total.shape, out_type),
        compiler_params=SMALL,
        cost_estimate=cost(us),
    )(left, piece, total)


def keys_of(ref):
    if len(ref.shape) == 2:
        return ref[:ROWS, :]
    return jnp.concatenate([ref[0, :ROWS, :], ref[1, :ROWS, :]], axis=0)


def values_of(ref):
    if len(ref.shape) == 2:
        return jnp.concatenate([ref[ROWS : ROWS + HEAD, :], ref[ROWS + HEAD :, :]], axis=1)
    return jnp.concatenate(
        [
            ref[0, ROWS : ROWS + HEAD, :],
            ref[0, ROWS + HEAD :, :],
            ref[1, ROWS : ROWS + HEAD, :],
            ref[1, ROWS + HEAD :, :],
        ],
        axis=1,
    )


def queries_of(q_refs, group):
    return jnp.concatenate(
        [q_refs[d][h * HEAD : (h + 1) * HEAD, :] for d in group for h in range(GROUP)], axis=1
    )


def fold(s):
    return jnp.sum(s.reshape(s.shape[0] // 8, 8, s.shape[1]), axis=0)


def attend_body(kinds, first, pairs, where_ref, *refs):
    last = pairs is not None
    pairs = list(range(NX // 2)) if pairs is None else pairs
    q_refs, refs = refs[:NX], refs[NX:]
    many = sum(2 if name == "both" else 1 for name, _ in kinds)
    kv_refs, refs = list(refs[:many]), refs[many:]
    if not first:
        old, refs = refs[:3], refs[3:]
    if last:
        out_refs, refs = refs[: 2 * len(pairs)], refs[2 * len(pairs) :]
    m_ref, l_ref, acc_ref = refs
    z, y, x = where_ref[0], where_ref[1], where_ref[2]
    if first:
        m_ref[...] = jnp.full(m_ref.shape, NEG, F32)
        l_ref[...] = jnp.zeros(l_ref.shape, F32)
        acc_ref[...] = jnp.zeros(acc_ref.shape, F32)
    else:
        for pair in pairs:
            cols = slice(pair * PAIR, (pair + 1) * PAIR)
            for new_ref, old_ref in zip((m_ref, l_ref, acc_ref), old):
                new_ref[:, cols] = old_ref[:, cols]

    def diagonal(d, ref):
        cols = slice(d * WIDE, (d + 1) * WIDE)

        def update():
            q = queries_of(q_refs, [d])
            s = jnp.dot(keys_of(ref), q, preferred_element_type=F32)
            if d == 0:
                key = lax.broadcasted_iota(jnp.int32, s.shape, 0)
                query = lax.broadcasted_iota(jnp.int32, s.shape, 1) % ROWS
                seen = key <= query
                s = jnp.where(seen, s, NEG)
            top = jnp.max(s, axis=0, keepdims=True)
            p = jnp.exp2((s - top) * C2)
            if d == 0:
                p = jnp.where(seen, p, 0.0)
            m_ref[:, cols] = top
            l_ref[:, cols] = fold(p)
            acc_ref[:, cols] = jnp.dot(values_of(ref), p.astype(BF), preferred_element_type=F32)

        if d == 0:
            update()
        else:
            pl.when(x + d < NX)(update)

    def whole(*blocks):
        keys = jnp.concatenate([keys_of(b) for b in blocks], axis=0)
        values = jnp.concatenate([values_of(b) for b in blocks], axis=1)
        for pair in pairs:
            cols = slice(pair * PAIR, (pair + 1) * PAIR)
            q = queries_of(q_refs, [2 * pair, 2 * pair + 1])
            s = jnp.dot(keys, q, preferred_element_type=F32)
            m_old = m_ref[:, cols]
            m_new = jnp.maximum(m_old, jnp.max(s, axis=0, keepdims=True))
            p = jnp.exp2((s - m_new) * C2)
            total = fold(p)
            add = jnp.dot(values, p.astype(BF), preferred_element_type=F32)
            factor = jnp.exp2((m_old - m_new) * C2)
            m_ref[:, cols] = m_new
            l_ref[:, cols] = l_ref[:, cols] * factor + total
            acc_ref[:, cols] = acc_ref[:, cols] * factor + add

    for name, steps in kinds:
        ref = kv_refs.pop(0)
        if name == "own":
            for d in range(NX):
                diagonal(d, ref)
        elif name == "other":
            pl.when(y == 1)(functools.partial(whole, ref))
        elif name == "up":
            pl.when(z >= steps)(functools.partial(whole, ref))
        else:
            below = kv_refs.pop(0)
            pl.when(z >= NZ - steps)(functools.partial(whole, ref, below))
            pl.when((z >= steps) & (z < NZ - steps))(functools.partial(whole, ref))

    if last:
        for place_at, d in enumerate([d for pair in pairs for d in (2 * pair, 2 * pair + 1)]):
            out_ref = out_refs[place_at]
            tops, totals = [], []
            for h in range(GROUP):
                cols = slice((d * GROUP + h) * ROWS, (d * GROUP + h + 1) * ROWS)
                total = jnp.sum(l_ref[:, cols], axis=0, keepdims=True)
                scale = jnp.where(total > 0.0, 1.0 / total, 0.0)
                out_ref[h * HEAD : (h + 1) * HEAD, :] = (acc_ref[:, cols] * scale).astype(BF)
                tops.append(m_ref[:, cols])
                totals.append(total)
            flat = jnp.concatenate(tops + totals, axis=0)
            hi = flat.astype(BF).astype(F32)
            mid = (flat - hi).astype(BF).astype(F32)
            low = flat - hi - mid
            packed = jnp.concatenate([hi, mid, low, jnp.zeros_like(flat)], axis=0)
            out_ref[GROUP * HEAD :, :] = packed.astype(BF)


STATE = [(1, NX * WIDE), (8, NX * WIDE), (HEAD, NX * WIDE)]


def attend(where, queries, blocks, state, pairs, us):
    kinds = [k for k, _ in blocks]
    first = state is None
    operands = [*queries, *[a for _, held in blocks for a in held]] + ([] if first else list(state))
    if pairs is not None:
        shapes = [jax.ShapeDtypeStruct((OUT_ROWS, ROWS), BF)] * (2 * len(pairs))
        scratch = [pltpu.VMEM(s, F32) for s in STATE]
    else:
        shapes = [jax.ShapeDtypeStruct(s, F32) for s in STATE]
        scratch = []
    return pl.pallas_call(
        functools.partial(attend_body, kinds, first, pairs),
        in_specs=[IN_SMEM] + [IN_VMEM] * len(operands),
        out_specs=[IN_VMEM] * len(shapes),
        out_shape=shapes,
        scratch_shapes=scratch,
        compiler_params=LARGE,
        cost_estimate=cost(us),
    )(where, *operands)


def combine_body(*refs):
    part_refs, out_ref = refs[:NX], refs[NX]
    tops, totals = [], []
    for ref in part_refs:
        packed = ref[GROUP * HEAD :, :].astype(F32)
        flat = packed[:8] + packed[8:16] + packed[16:24]
        tops.append(flat[:GROUP])
        totals.append(flat[GROUP:])
    best = functools.reduce(jnp.maximum, tops)
    weights = [t * jnp.exp2((m - best) * C2) for m, t in zip(tops, totals)]
    inverse = 1.0 / functools.reduce(jnp.add, weights)
    weights = [w * inverse for w in weights]
    for h in range(GROUP):
        rows = slice(h * HEAD, (h + 1) * HEAD)
        mixed = functools.reduce(
            jnp.add,
            [ref[rows, :].astype(F32) * w[h : h + 1] for ref, w in zip(part_refs, weights)],
        )
        out_ref[:, rows] = mixed.T.astype(BF)


def combine(parts):
    return pl.pallas_call(
        combine_body,
        in_specs=[IN_VMEM] * NX,
        out_specs=IN_VMEM,
        out_shape=jax.ShapeDtypeStruct((ROWS, GROUP * HEAD), BF),
        compiler_params=SMALL,
        cost_estimate=cost(1),
    )(*parts)


def local(tokens, w_query, key_matrix, value_matrix, w_output):
    c = lax.axis_index("ctx").astype(jnp.int32)
    h = lax.axis_index("head").astype(jnp.int32)
    where = jnp.stack([c // (NY * NX), (c // NX) % NY, c % NX])
    near = jnp.stack([h, h ^ 1])
    far = jnp.stack([h ^ 2, h ^ 3])
    width = tokens.shape[1]
    t_core = lax.ppermute(tokens, "head", swap(1))
    t_chip = lax.ppermute(tokens, "head", swap(2))
    slices = columns_apart(w_output, width)
    sums, rest, done = project_near(
        near, far, tokens, t_core, (w_query, key_matrix, value_matrix), [slices], 12
    )
    t_chip, done = lax.optimization_barrier((t_chip, done))
    t_far = lax.ppermute(t_chip, "head", swap(1))
    query = project_far(
        t_chip, t_far, rest[:1], sums[:1], [], store_turned, (GROUP * HEAD, ROWS), 2
    )
    own = project_far(
        t_chip, t_far, rest[1:], sums[1:], [query], store_keys_values, (2 * ROWS, HEAD), 2
    )
    other = lax.ppermute(own, "ctx", shift(0, 1, 0))
    queries = [query] + [lax.ppermute(query, "ctx", shift(0, 0, -d)) for d in range(1, NX)]
    slices, _ = lax.optimization_barrier((slices, other))
    pieces = lax.all_to_all(slices, "head", 0, 0, tiled=True)
    level = pair_up(own, other, queries)

    up = down = level
    state = None
    blocks = [(("own", 0), [own]), (("other", 0), [other])]
    for s in range(1, 5):
        up = lax.ppermute(up, "ctx", shift(1, 0, 0))
        if s < 4:
            down = lax.ppermute(down, "ctx", shift(-1, 0, 0))
        if s > 1:
            state = attend(where, queries, blocks, state, None, 6)
            up, down, state = lax.optimization_barrier((up, down, state))
            blocks = [(("both", s - 1), [last_up, last_down])]
        last_up, last_down = up, down
    blocks += [(("up", 4), [up])]
    parts = [None] * NX
    parts[2], parts[3] = attend(where, queries, blocks, state, [1], 6)
    sent = [None] * NX
    for d in (2, 3):
        sent[d] = lax.ppermute(parts[d], "ctx", shift(0, 0, d))
    parts[0], parts[1] = attend(where, queries, blocks, state, [0], 6)
    sent[0] = parts[0]
    sent[1] = lax.ppermute(parts[1], "ctx", shift(0, 0, 1))
    attended = combine(sent)
    a_chip = lax.ppermute(attended, "head", swap(2))
    a_core = lax.ppermute(attended, "head", swap(1))
    total, rest = products_near(near, far, [attended, a_core], pieces, 3)
    total, a_chip = lax.optimization_barrier((total, a_chip))
    a_far = lax.ppermute(a_chip, "head", swap(1))
    total = product(a_chip, rest[0], total, F32, 2)
    return product(a_far, rest[1], total, BF, 2)


def solution(mesh):
    return jax.shard_map(
        local,
        mesh=mesh,
        in_specs=(
            P("ctx", "head"),
            P(None, "head"),
            P(None, "head"),
            P(None, "head"),
            P("head", None),
        ),
        out_specs=P("ctx", "head"),
        check_vma=False,
    )
```

```python
import functools

import jax
import jax.numpy as jnp
from jax import lax
from jax.experimental import pallas as pl
from jax.experimental.pallas import tpu as pltpu
from jax.sharding import PartitionSpec as P

HEAD = 128
GROUP = 4
NZ, NY, NX = 8, 2, 4
ROWS = 256
WIDE = GROUP * ROWS
STAT_ROWS = 32
OUT_ROWS = GROUP * HEAD + STAT_ROWS
NEG = -1e30
C2 = HEAD**-0.5 * 1.4426950408889634
BF = jnp.bfloat16
F32 = jnp.float32
MIB = 1024 * 1024
SMALL = pltpu.CompilerParams(vmem_limit_bytes=16 * MIB)
LARGE = pltpu.CompilerParams(vmem_limit_bytes=40 * MIB)
IN_VMEM = pl.BlockSpec(memory_space=pltpu.VMEM)
IN_SMEM = pl.BlockSpec(memory_space=pltpu.SMEM)
IN_HBM = pl.BlockSpec(memory_space=pltpu.HBM)
ANYWHERE = pl.BlockSpec(memory_space=pl.ANY)


def place(z, y, x):
    return (z % NZ) * (NY * NX) + (y % NY) * NX + x % NX


def shift(dz, dy, dx):
    return [
        (place(z, y, x), place(z + dz, y + dy, x + dx))
        for z in range(NZ)
        for y in range(NY)
        for x in range(NX)
    ]


def swap(bit):
    return [(h, h ^ bit) for h in range(4)]


def cost(us):
    return pl.CostEstimate(
        flops=int(us * 10**9), bytes_accessed=int(us * 3 * 10**6), transcendentals=0
    )


def project_near(near, far, first, second, weights, after, us):
    depth = first.shape[1]
    count = len(weights)

    def rows(blocks_ref, step):
        return pl.ds(pl.multiple_of(blocks_ref[step] * depth, depth), depth)

    def body(near_ref, far_ref, first_ref, second_ref, *refs):
        w_refs, refs = refs[:count], refs[count + len(after) :]
        s_refs, f_refs, done_ref = refs[:count], refs[count : 2 * count], refs[-1]
        done_ref[...] = jnp.zeros(done_ref.shape, F32)
        for n in range(count):
            s_refs[n][...] = jnp.dot(
                first_ref[...], w_refs[n][rows(near_ref, 0), :], preferred_element_type=F32
            ) + jnp.dot(
                second_ref[...], w_refs[n][rows(near_ref, 1), :], preferred_element_type=F32
            )
            for step in range(2):
                f_refs[n][step] = w_refs[n][rows(far_ref, step), :]

    widths = [w.shape[1] for w in weights]
    out = pl.pallas_call(
        body,
        in_specs=[IN_SMEM] * 2 + [IN_VMEM] * (2 + count) + [ANYWHERE] * len(after),
        out_specs=[IN_VMEM] * (2 * count + 1),
        out_shape=[jax.ShapeDtypeStruct((first.shape[0], n), F32) for n in widths]
        + [jax.ShapeDtypeStruct((2, depth, n), BF) for n in widths]
        + [jax.ShapeDtypeStruct((8, HEAD), F32)],
        compiler_params=SMALL,
        cost_estimate=cost(us),
    )(near, far, first, second, *weights, *after)
    return out[:count], out[count : 2 * count], out[-1]


def project_far(first, second, weights, sums, after, finish, shape, us):
    count = len(weights)

    def body(first_ref, second_ref, *refs):
        w_refs, s_refs = refs[:count], refs[count : 2 * count]
        totals = []
        for n in range(count):
            total = s_refs[n][...] + jnp.dot(
                first_ref[...], w_refs[n][0], preferred_element_type=F32
            )
            totals.append(
                total + jnp.dot(second_ref[...], w_refs[n][1], preferred_element_type=F32)
            )
        finish(totals, refs[-1])

    return pl.pallas_call(
        body,
        in_specs=[IN_VMEM] * (2 + 2 * count) + [ANYWHERE] * len(after),
        out_specs=IN_VMEM,
        out_shape=jax.ShapeDtypeStruct(shape, BF),
        compiler_params=SMALL,
        cost_estimate=cost(us),
    )(first, second, *weights, *sums, *after)


def pair_up(own, other, after):
    def body(own_ref, other_ref, *refs):
        refs[-1][0] = own_ref[...]
        refs[-1][1] = other_ref[...]

    return pl.pallas_call(
        body,
        in_specs=[IN_VMEM] * 2 + [ANYWHERE] * len(after),
        out_specs=IN_VMEM,
        out_shape=jax.ShapeDtypeStruct((2,) + own.shape, own.dtype),
        compiler_params=SMALL,
        cost_estimate=cost(1),
    )(own, other, *after)


def columns_apart(w, width):
    count = w.shape[1] // width

    def body(w_ref, o_ref, sem):
        copies = [
            pltpu.make_async_copy(
                w_ref.at[:, pl.ds(n * width, width)], o_ref.at[n], sem.at[n]
            )
            for n in range(count)
        ]
        for c in copies:
            c.start()
        for c in copies:
            c.wait()

    return pl.pallas_call(
        body,
        in_specs=[IN_HBM],
        out_specs=IN_HBM,
        out_shape=jax.ShapeDtypeStruct((count, w.shape[0], width), w.dtype),
        scratch_shapes=[pltpu.SemaphoreType.DMA((count,))],
        compiler_params=SMALL,
        cost_estimate=cost(3),
    )(w)


def store_keys_values(totals, out):
    keys, values = totals
    turned = values.T.astype(BF)
    out[:ROWS] = keys.astype(BF)
    out[ROWS : ROWS + HEAD] = turned[:, :HEAD]
    out[ROWS + HEAD :] = turned[:, HEAD:]


def store_turned(totals, out):
    out[...] = totals[0].T.astype(BF)


def products_near(near, far, lefts, pieces, us):
    count = len(lefts)

    def body(near_ref, far_ref, pieces_ref, *refs):
        o_ref, rest_refs = refs[count], refs[count + 1 : count + 3]
        held, sem = refs[-2:]
        copies = [
            pltpu.make_async_copy(pieces_ref.at[near_ref[n]], held.at[n], sem.at[n])
            for n in range(count)
        ]
        copies += [
            pltpu.make_async_copy(pieces_ref.at[far_ref[n]], rest_refs[n], sem.at[count + n])
            for n in range(2)
        ]
        for c in copies:
            c.start()
        total = None
        for n in range(count):
            copies[n].wait()
            term = jnp.dot(refs[n][...], held[n], preferred_element_type=F32)
            total = term if total is None else total + term
        o_ref[...] = total
        for c in copies[count:]:
            c.wait()

    piece = jax.ShapeDtypeStruct(pieces.shape[1:], BF)
    total, *rest = pl.pallas_call(
        body,
        in_specs=[IN_SMEM] * 2 + [IN_HBM] + [IN_VMEM] * count,
        out_specs=[IN_VMEM] * 3,
        out_shape=[jax.ShapeDtypeStruct((lefts[0].shape[0], pieces.shape[2]), F32), piece, piece],
        scratch_shapes=[
            pltpu.VMEM((count,) + pieces.shape[1:], BF),
            pltpu.SemaphoreType.DMA((count + 2,)),
        ],
        compiler_params=SMALL,
        cost_estimate=cost(us),
    )(near, far, pieces, *lefts)
    return total, rest


def product(left, piece, total, out_type, us):
    def body(left_ref, piece_ref, total_ref, o_ref):
        term = jnp.dot(left_ref[...], piece_ref[...], preferred_element_type=F32)
        o_ref[...] = (total_ref[...] + term).astype(out_type)

    return pl.pallas_call(
        body,
        in_specs=[IN_VMEM] * 3,
        out_specs=IN_VMEM,
        out_shape=jax.ShapeDtypeStruct(total.shape, out_type),
        compiler_params=SMALL,
        cost_estimate=cost(us),
    )(left, piece, total)


def keys_of(ref):
    if len(ref.shape) == 2:
        return ref[:ROWS, :]
    return jnp.concatenate([ref[0, :ROWS, :], ref[1, :ROWS, :]], axis=0)


def values_of(ref):
    if len(ref.shape) == 2:
        return jnp.concatenate([ref[ROWS : ROWS + HEAD, :], ref[ROWS + HEAD :, :]], axis=1)
    return jnp.concatenate(
        [
            ref[0, ROWS : ROWS + HEAD, :],
            ref[0, ROWS + HEAD :, :],
            ref[1, ROWS : ROWS + HEAD, :],
            ref[1, ROWS + HEAD :, :],
        ],
        axis=1,
    )


def queries_of(q_refs, group):
    return jnp.concatenate(
        [q_refs[d][h * HEAD : (h + 1) * HEAD, :] for d in group for h in range(GROUP)], axis=1
    )


def fold(s):
    return jnp.sum(s.reshape(s.shape[0] // 8, 8, s.shape[1]), axis=0)


def attend_body(kinds, first, groups, where_ref, *refs):
    last = groups is not None
    groups = [(0, 1), (2, 3)] if groups is None else groups
    places = [d for group in groups for d in group]
    spans = [slice(group[0] * WIDE, (group[-1] + 1) * WIDE) for group in groups]
    q_refs, refs = refs[:NX], refs[NX:]
    many = sum(2 if name == "both" else 1 for name, _ in kinds)
    kv_refs, refs = list(refs[:many]), refs[many:]
    if not first:
        old, refs = refs[:3], refs[3:]
    if last:
        out_refs, refs = refs[: len(places)], refs[len(places) :]
    m_ref, l_ref, acc_ref = refs
    z, y, x = where_ref[0], where_ref[1], where_ref[2]
    if first:
        m_ref[...] = jnp.full(m_ref.shape, NEG, F32)
        l_ref[...] = jnp.zeros(l_ref.shape, F32)
        acc_ref[...] = jnp.zeros(acc_ref.shape, F32)
    else:
        for cols in spans:
            for new_ref, old_ref in zip((m_ref, l_ref, acc_ref), old):
                new_ref[:, cols] = old_ref[:, cols]

    def diagonal(d, ref):
        cols = slice(d * WIDE, (d + 1) * WIDE)

        def update():
            q = queries_of(q_refs, [d])
            s = jnp.dot(keys_of(ref), q, preferred_element_type=F32)
            if d == 0:
                key = lax.broadcasted_iota(jnp.int32, s.shape, 0)
                query = lax.broadcasted_iota(jnp.int32, s.shape, 1) % ROWS
                seen = key <= query
                s = jnp.where(seen, s, NEG)
            top = jnp.max(s, axis=0, keepdims=True)
            p = jnp.exp2((s - top) * C2)
            if d == 0:
                p = jnp.where(seen, p, 0.0)
            m_ref[:, cols] = top
            l_ref[:, cols] = fold(p)
            acc_ref[:, cols] = jnp.dot(values_of(ref), p.astype(BF), preferred_element_type=F32)

        if d == 0:
            update()
        else:
            pl.when(x + d < NX)(update)

    def whole(*blocks):
        keys = jnp.concatenate([keys_of(b) for b in blocks], axis=0)
        values = jnp.concatenate([values_of(b) for b in blocks], axis=1)
        for group, cols in zip(groups, spans):
            q = queries_of(q_refs, group)
            s = jnp.dot(keys, q, preferred_element_type=F32)
            m_old = m_ref[:, cols]
            m_new = jnp.maximum(m_old, jnp.max(s, axis=0, keepdims=True))
            p = jnp.exp2((s - m_new) * C2)
            total = fold(p)
            add = jnp.dot(values, p.astype(BF), preferred_element_type=F32)
            factor = jnp.exp2((m_old - m_new) * C2)
            m_ref[:, cols] = m_new
            l_ref[:, cols] = l_ref[:, cols] * factor + total
            acc_ref[:, cols] = acc_ref[:, cols] * factor + add

    for name, steps in kinds:
        ref = kv_refs.pop(0)
        if name == "own":
            for d in range(NX):
                diagonal(d, ref)
        elif name == "other":
            pl.when(y == 1)(functools.partial(whole, ref))
        elif name == "up":
            pl.when(z >= steps)(functools.partial(whole, ref))
        else:
            below = kv_refs.pop(0)
            pl.when(z >= NZ - steps)(functools.partial(whole, ref, below))
            pl.when((z >= steps) & (z < NZ - steps))(functools.partial(whole, ref))

    if last:
        for place_at, d in enumerate(places):
            out_ref = out_refs[place_at]
            tops, totals = [], []
            for h in range(GROUP):
                cols = slice((d * GROUP + h) * ROWS, (d * GROUP + h + 1) * ROWS)
                total = jnp.sum(l_ref[:, cols], axis=0, keepdims=True)
                scale = jnp.where(total > 0.0, 1.0 / total, 0.0)
                out_ref[h * HEAD : (h + 1) * HEAD, :] = (acc_ref[:, cols] * scale).astype(BF)
                tops.append(m_ref[:, cols])
                totals.append(total)
            flat = jnp.concatenate(tops + totals, axis=0)
            hi = flat.astype(BF).astype(F32)
            mid = (flat - hi).astype(BF).astype(F32)
            low = flat - hi - mid
            packed = jnp.concatenate([hi, mid, low, jnp.zeros_like(flat)], axis=0)
            out_ref[GROUP * HEAD :, :] = packed.astype(BF)


STATE = [(1, NX * WIDE), (8, NX * WIDE), (HEAD, NX * WIDE)]


def attend(where, queries, blocks, state, groups, us):
    kinds = [k for k, _ in blocks]
    first = state is None
    operands = [*queries, *[a for _, held in blocks for a in held]] + ([] if first else list(state))
    if groups is not None:
        shapes = [jax.ShapeDtypeStruct((OUT_ROWS, ROWS), BF)] * sum(map(len, groups))
        scratch = [pltpu.VMEM(s, F32) for s in STATE]
    else:
        shapes = [jax.ShapeDtypeStruct(s, F32) for s in STATE]
        scratch = []
    return pl.pallas_call(
        functools.partial(attend_body, kinds, first, groups),
        in_specs=[IN_SMEM] + [IN_VMEM] * len(operands),
        out_specs=[IN_VMEM] * len(shapes),
        out_shape=shapes,
        scratch_shapes=scratch,
        compiler_params=LARGE,
        cost_estimate=cost(us),
    )(where, *operands)


def combine_body(*refs):
    part_refs, out_ref = refs[:NX], refs[NX]
    tops, totals = [], []
    for ref in part_refs:
        packed = ref[GROUP * HEAD :, :].astype(F32)
        flat = packed[:8] + packed[8:16] + packed[16:24]
        tops.append(flat[:GROUP])
        totals.append(flat[GROUP:])
    best = functools.reduce(jnp.maximum, tops)
    weights = [t * jnp.exp2((m - best) * C2) for m, t in zip(tops, totals)]
    inverse = 1.0 / functools.reduce(jnp.add, weights)
    weights = [w * inverse for w in weights]
    for h in range(GROUP):
        rows = slice(h * HEAD, (h + 1) * HEAD)
        mixed = functools.reduce(
            jnp.add,
            [ref[rows, :].astype(F32) * w[h : h + 1] for ref, w in zip(part_refs, weights)],
        )
        out_ref[:, rows] = mixed.T.astype(BF)


def combine(parts):
    return pl.pallas_call(
        combine_body,
        in_specs=[IN_VMEM] * NX,
        out_specs=IN_VMEM,
        out_shape=jax.ShapeDtypeStruct((ROWS, GROUP * HEAD), BF),
        compiler_params=SMALL,
        cost_estimate=cost(1),
    )(*parts)


def local(tokens, w_query, key_matrix, value_matrix, w_output):
    c = lax.axis_index("ctx").astype(jnp.int32)
    h = lax.axis_index("head").astype(jnp.int32)
    where = jnp.stack([c // (NY * NX), (c // NX) % NY, c % NX])
    near = jnp.stack([h, h ^ 1])
    far = jnp.stack([h ^ 2, h ^ 3])
    width = tokens.shape[1]
    t_core = lax.ppermute(tokens, "head", swap(1))
    t_chip = lax.ppermute(tokens, "head", swap(2))
    slices = columns_apart(w_output, width)
    sums, rest, done = project_near(
        near, far, tokens, t_core, (w_query, key_matrix, value_matrix), [slices], 12
    )
    t_chip, done = lax.optimization_barrier((t_chip, done))
    t_far = lax.ppermute(t_chip, "head", swap(1))
    query = project_far(
        t_chip, t_far, rest[:1], sums[:1], [done], store_turned, (GROUP * HEAD, ROWS), 2
    )
    own = project_far(
        t_chip, t_far, rest[1:], sums[1:], [query], store_keys_values, (2 * ROWS, HEAD), 2
    )
    other = lax.ppermute(own, "ctx", shift(0, 1, 0))
    queries = [query] + [lax.ppermute(query, "ctx", shift(0, 0, -d)) for d in range(1, NX)]
    slices, _ = lax.optimization_barrier((slices, other))
    pieces = lax.all_to_all(slices, "head", 0, 0, tiled=True)
    level = pair_up(own, other, queries)

    up = down = level
    state = None
    blocks = [(("own", 0), [own]), (("other", 0), [other])]
    for s in range(1, 5):
        up = lax.ppermute(up, "ctx", shift(1, 0, 0))
        if s < 4:
            down = lax.ppermute(down, "ctx", shift(-1, 0, 0))
        if s > 1:
            state = attend(where, queries, blocks, state, None, 6)
            up, down, state = lax.optimization_barrier((up, down, state))
            blocks = [(("both", s - 1), [last_up, last_down])]
        last_up, last_down = up, down
    blocks += [(("up", 4), [up])]
    sent = [None] * NX
    for group in ((2, 3), (1,), (0,)):
        parts = attend(where, queries, blocks, state, [group], 3 * len(group))
        for d, part in zip(group, parts):
            sent[d] = lax.ppermute(part, "ctx", shift(0, 0, d)) if d else part
    attended = combine(sent)
    a_chip = lax.ppermute(attended, "head", swap(2))
    a_core = lax.ppermute(attended, "head", swap(1))
    total, rest = products_near(near, far, [attended, a_core], pieces, 3)
    total, a_chip = lax.optimization_barrier((total, a_chip))
    a_far = lax.ppermute(a_chip, "head", swap(1))
    total = product(a_chip, rest[0], total, F32, 2)
    return product(a_far, rest[1], total, BF, 2)


def solution(mesh):
    return jax.shard_map(
        local,
        mesh=mesh,
        in_specs=(
            P("ctx", "head"),
            P(None, "head"),
            P(None, "head"),
            P(None, "head"),
            P("head", None),
        ),
        out_specs=P("ctx", "head"),
        check_vma=False,
    )
```

```python
import functools

import jax
import jax.numpy as jnp
from jax import lax
from jax.experimental import pallas as pl
from jax.experimental.pallas import tpu as pltpu
from jax.sharding import PartitionSpec as P

HEAD = 128
GROUP = 4
NZ, NY, NX = 8, 2, 4
ROWS = 256
WIDE = GROUP * ROWS
STAT_ROWS = 32
OUT_ROWS = GROUP * HEAD + STAT_ROWS
NEG = -1e30
C2 = HEAD**-0.5 * 1.4426950408889634
BF = jnp.bfloat16
F32 = jnp.float32
MIB = 1024 * 1024
SMALL = pltpu.CompilerParams(vmem_limit_bytes=16 * MIB)
LARGE = pltpu.CompilerParams(vmem_limit_bytes=40 * MIB)
IN_VMEM = pl.BlockSpec(memory_space=pltpu.VMEM)
IN_SMEM = pl.BlockSpec(memory_space=pltpu.SMEM)
IN_HBM = pl.BlockSpec(memory_space=pltpu.HBM)
ANYWHERE = pl.BlockSpec(memory_space=pl.ANY)


def place(z, y, x):
    return (z % NZ) * (NY * NX) + (y % NY) * NX + x % NX


def shift(dz, dy, dx):
    return [
        (place(z, y, x), place(z + dz, y + dy, x + dx))
        for z in range(NZ)
        for y in range(NY)
        for x in range(NX)
    ]


def swap(bit):
    return [(h, h ^ bit) for h in range(4)]


def cost(us):
    return pl.CostEstimate(
        flops=int(us * 10**9), bytes_accessed=int(us * 3 * 10**6), transcendentals=0
    )


def project_near(near, far, first, second, weights, after, us):
    depth = first.shape[1]
    count = len(weights)

    def rows(blocks_ref, step):
        return pl.ds(pl.multiple_of(blocks_ref[step] * depth, depth), depth)

    def body(near_ref, far_ref, first_ref, second_ref, *refs):
        w_refs, refs = refs[:count], refs[count + len(after) :]
        s_refs, f_refs, done_ref = refs[:count], refs[count : 2 * count], refs[-1]
        done_ref[...] = jnp.zeros(done_ref.shape, F32)
        for n in range(count):
            s_refs[n][...] = jnp.dot(
                first_ref[...], w_refs[n][rows(near_ref, 0), :], preferred_element_type=F32
            ) + jnp.dot(
                second_ref[...], w_refs[n][rows(near_ref, 1), :], preferred_element_type=F32
            )
            for step in range(2):
                f_refs[n][step] = w_refs[n][rows(far_ref, step), :]

    widths = [w.shape[1] for w in weights]
    out = pl.pallas_call(
        body,
        in_specs=[IN_SMEM] * 2 + [IN_VMEM] * (2 + count) + [ANYWHERE] * len(after),
        out_specs=[IN_VMEM] * (2 * count + 1),
        out_shape=[jax.ShapeDtypeStruct((first.shape[0], n), F32) for n in widths]
        + [jax.ShapeDtypeStruct((2, depth, n), BF) for n in widths]
        + [jax.ShapeDtypeStruct((8, HEAD), F32)],
        compiler_params=SMALL,
        cost_estimate=cost(us),
    )(near, far, first, second, *weights, *after)
    return out[:count], out[count : 2 * count], out[-1]


def project_far(first, second, weights, sums, after, finish, shape, us):
    count = len(weights)

    def body(first_ref, second_ref, *refs):
        w_refs, s_refs = refs[:count], refs[count : 2 * count]
        totals = []
        for n in range(count):
            total = s_refs[n][...] + jnp.dot(
                first_ref[...], w_refs[n][0], preferred_element_type=F32
            )
            totals.append(
                total + jnp.dot(second_ref[...], w_refs[n][1], preferred_element_type=F32)
            )
        finish(totals, refs[-1])

    return pl.pallas_call(
        body,
        in_specs=[IN_VMEM] * (2 + 2 * count) + [ANYWHERE] * len(after),
        out_specs=IN_VMEM,
        out_shape=jax.ShapeDtypeStruct(shape, BF),
        compiler_params=SMALL,
        cost_estimate=cost(us),
    )(first, second, *weights, *sums, *after)


def pair_up(own, other, after):
    def body(own_ref, other_ref, *refs):
        refs[-1][0] = own_ref[...]
        refs[-1][1] = other_ref[...]

    return pl.pallas_call(
        body,
        in_specs=[IN_VMEM] * 2 + [ANYWHERE] * len(after),
        out_specs=IN_VMEM,
        out_shape=jax.ShapeDtypeStruct((2,) + own.shape, own.dtype),
        compiler_params=SMALL,
        cost_estimate=cost(1),
    )(own, other, *after)


def columns_apart(w, width):
    count = w.shape[1] // width

    def body(w_ref, o_ref, sem):
        copies = [
            pltpu.make_async_copy(
                w_ref.at[:, pl.ds(n * width, width)], o_ref.at[n], sem.at[n]
            )
            for n in range(count)
        ]
        for c in copies:
            c.start()
        for c in copies:
            c.wait()

    return pl.pallas_call(
        body,
        in_specs=[IN_HBM],
        out_specs=IN_HBM,
        out_shape=jax.ShapeDtypeStruct((count, w.shape[0], width), w.dtype),
        scratch_shapes=[pltpu.SemaphoreType.DMA((count,))],
        compiler_params=SMALL,
        cost_estimate=cost(3),
    )(w)


def store_keys_values(totals, out):
    keys, values = totals
    turned = values.T.astype(BF)
    out[:ROWS] = keys.astype(BF)
    out[ROWS : ROWS + HEAD] = turned[:, :HEAD]
    out[ROWS + HEAD :] = turned[:, HEAD:]


def store_turned(totals, out):
    out[...] = totals[0].T.astype(BF)


def products_near(near, far, lefts, pieces, us):
    count = len(lefts)

    def body(near_ref, far_ref, pieces_ref, *refs):
        o_ref, rest_refs = refs[count], refs[count + 1 : count + 3]
        held, sem = refs[-2:]
        copies = [
            pltpu.make_async_copy(pieces_ref.at[near_ref[n]], held.at[n], sem.at[n])
            for n in range(count)
        ]
        copies += [
            pltpu.make_async_copy(pieces_ref.at[far_ref[n]], rest_refs[n], sem.at[count + n])
            for n in range(2)
        ]
        for c in copies:
            c.start()
        total = None
        for n in range(count):
            copies[n].wait()
            term = jnp.dot(refs[n][...], held[n], preferred_element_type=F32)
            total = term if total is None else total + term
        o_ref[...] = total
        for c in copies[count:]:
            c.wait()

    piece = jax.ShapeDtypeStruct(pieces.shape[1:], BF)
    total, *rest = pl.pallas_call(
        body,
        in_specs=[IN_SMEM] * 2 + [IN_HBM] + [IN_VMEM] * count,
        out_specs=[IN_VMEM] * 3,
        out_shape=[jax.ShapeDtypeStruct((lefts[0].shape[0], pieces.shape[2]), F32), piece, piece],
        scratch_shapes=[
            pltpu.VMEM((count,) + pieces.shape[1:], BF),
            pltpu.SemaphoreType.DMA((count + 2,)),
        ],
        compiler_params=SMALL,
        cost_estimate=cost(us),
    )(near, far, pieces, *lefts)
    return total, rest


def product(left, piece, total, out_type, us):
    def body(left_ref, piece_ref, total_ref, o_ref):
        term = jnp.dot(left_ref[...], piece_ref[...], preferred_element_type=F32)
        o_ref[...] = (total_ref[...] + term).astype(out_type)

    return pl.pallas_call(
        body,
        in_specs=[IN_VMEM] * 3,
        out_specs=IN_VMEM,
        out_shape=jax.ShapeDtypeStruct(total.shape, out_type),
        compiler_params=SMALL,
        cost_estimate=cost(us),
    )(left, piece, total)


def keys_of(ref):
    if len(ref.shape) == 2:
        return ref[:ROWS, :]
    return jnp.concatenate([ref[0, :ROWS, :], ref[1, :ROWS, :]], axis=0)


def values_of(ref):
    if len(ref.shape) == 2:
        return jnp.concatenate([ref[ROWS : ROWS + HEAD, :], ref[ROWS + HEAD :, :]], axis=1)
    return jnp.concatenate(
        [
            ref[0, ROWS : ROWS + HEAD, :],
            ref[0, ROWS + HEAD :, :],
            ref[1, ROWS : ROWS + HEAD, :],
            ref[1, ROWS + HEAD :, :],
        ],
        axis=1,
    )


def queries_of(q_refs, group):
    return jnp.concatenate(
        [q_refs[d][h * HEAD : (h + 1) * HEAD, :] for d in group for h in range(GROUP)], axis=1
    )


def fold(s):
    return jnp.sum(s.reshape(s.shape[0] // 8, 8, s.shape[1]), axis=0)


def attend_body(kinds, first, groups, where_ref, *refs):
    last = groups is not None
    groups = [(0, 1), (2, 3)] if groups is None else groups
    places = [d for group in groups for d in group]
    spans = [slice(group[0] * WIDE, (group[-1] + 1) * WIDE) for group in groups]
    q_refs, refs = refs[:NX], refs[NX:]
    many = sum(2 if name == "both" else 1 for name, _ in kinds)
    kv_refs, refs = list(refs[:many]), refs[many:]
    if not first:
        old, refs = refs[:3], refs[3:]
    if last:
        out_refs, refs = refs[: len(places)], refs[len(places) :]
    m_ref, l_ref, acc_ref = refs
    z, y, x = where_ref[0], where_ref[1], where_ref[2]
    if first:
        m_ref[...] = jnp.full(m_ref.shape, NEG, F32)
        l_ref[...] = jnp.zeros(l_ref.shape, F32)
        acc_ref[...] = jnp.zeros(acc_ref.shape, F32)
    else:
        for cols in spans:
            for new_ref, old_ref in zip((m_ref, l_ref, acc_ref), old):
                new_ref[:, cols] = old_ref[:, cols]

    def diagonal(d, ref):
        cols = slice(d * WIDE, (d + 1) * WIDE)

        def update():
            q = queries_of(q_refs, [d])
            s = jnp.dot(keys_of(ref), q, preferred_element_type=F32)
            if d == 0:
                key = lax.broadcasted_iota(jnp.int32, s.shape, 0)
                query = lax.broadcasted_iota(jnp.int32, s.shape, 1) % ROWS
                seen = key <= query
                s = jnp.where(seen, s, NEG)
            top = jnp.max(s, axis=0, keepdims=True)
            p = jnp.exp2((s - top) * C2)
            if d == 0:
                p = jnp.where(seen, p, 0.0)
            m_ref[:, cols] = top
            l_ref[:, cols] = fold(p)
            acc_ref[:, cols] = jnp.dot(values_of(ref), p.astype(BF), preferred_element_type=F32)

        if d == 0:
            update()
        else:
            pl.when(x + d < NX)(update)

    def whole(*blocks):
        keys = jnp.concatenate([keys_of(b) for b in blocks], axis=0)
        values = jnp.concatenate([values_of(b) for b in blocks], axis=1)
        for group, cols in zip(groups, spans):
            q = queries_of(q_refs, group)
            s = jnp.dot(keys, q, preferred_element_type=F32)
            m_old = m_ref[:, cols]
            m_new = jnp.maximum(m_old, jnp.max(s, axis=0, keepdims=True))
            p = jnp.exp2((s - m_new) * C2)
            total = fold(p)
            add = jnp.dot(values, p.astype(BF), preferred_element_type=F32)
            factor = jnp.exp2((m_old - m_new) * C2)
            m_ref[:, cols] = m_new
            l_ref[:, cols] = l_ref[:, cols] * factor + total
            acc_ref[:, cols] = acc_ref[:, cols] * factor + add

    for name, steps in kinds:
        ref = kv_refs.pop(0)
        if name == "own":
            for d in range(NX):
                diagonal(d, ref)
        elif name == "other":
            pl.when(y == 1)(functools.partial(whole, ref))
        elif name == "up":
            pl.when(z >= steps)(functools.partial(whole, ref))
        else:
            below = kv_refs.pop(0)
            pl.when(z >= NZ - steps)(functools.partial(whole, ref, below))
            pl.when((z >= steps) & (z < NZ - steps))(functools.partial(whole, ref))

    if last:
        for place_at, d in enumerate(places):
            out_ref = out_refs[place_at]
            tops, totals = [], []
            for h in range(GROUP):
                cols = slice((d * GROUP + h) * ROWS, (d * GROUP + h + 1) * ROWS)
                total = jnp.sum(l_ref[:, cols], axis=0, keepdims=True)
                scale = jnp.where(total > 0.0, 1.0 / total, 0.0)
                out_ref[h * HEAD : (h + 1) * HEAD, :] = (acc_ref[:, cols] * scale).astype(BF)
                tops.append(m_ref[:, cols])
                totals.append(total)
            flat = jnp.concatenate(tops + totals, axis=0)
            hi = flat.astype(BF).astype(F32)
            mid = (flat - hi).astype(BF).astype(F32)
            low = flat - hi - mid
            packed = jnp.concatenate([hi, mid, low, jnp.zeros_like(flat)], axis=0)
            out_ref[GROUP * HEAD :, :] = packed.astype(BF)


STATE = [(1, NX * WIDE), (8, NX * WIDE), (HEAD, NX * WIDE)]


def attend(where, queries, blocks, state, groups, us):
    kinds = [k for k, _ in blocks]
    first = state is None
    operands = [*queries, *[a for _, held in blocks for a in held]] + ([] if first else list(state))
    if groups is not None:
        shapes = [jax.ShapeDtypeStruct((OUT_ROWS, ROWS), BF)] * sum(map(len, groups))
        scratch = [pltpu.VMEM(s, F32) for s in STATE]
    else:
        shapes = [jax.ShapeDtypeStruct(s, F32) for s in STATE]
        scratch = []
    return pl.pallas_call(
        functools.partial(attend_body, kinds, first, groups),
        in_specs=[IN_SMEM] + [IN_VMEM] * len(operands),
        out_specs=[IN_VMEM] * len(shapes),
        out_shape=shapes,
        scratch_shapes=scratch,
        compiler_params=LARGE,
        cost_estimate=cost(us),
    )(where, *operands)


def combine_body(*refs):
    part_refs, out_ref = refs[:NX], refs[NX]
    tops, totals = [], []
    for ref in part_refs:
        packed = ref[GROUP * HEAD :, :].astype(F32)
        flat = packed[:8] + packed[8:16] + packed[16:24]
        tops.append(flat[:GROUP])
        totals.append(flat[GROUP:])
    best = functools.reduce(jnp.maximum, tops)
    weights = [t * jnp.exp2((m - best) * C2) for m, t in zip(tops, totals)]
    inverse = 1.0 / functools.reduce(jnp.add, weights)
    weights = [w * inverse for w in weights]
    for h in range(GROUP):
        rows = slice(h * HEAD, (h + 1) * HEAD)
        mixed = functools.reduce(
            jnp.add,
            [ref[rows, :].astype(F32) * w[h : h + 1] for ref, w in zip(part_refs, weights)],
        )
        out_ref[:, rows] = mixed.T.astype(BF)


def combine(parts):
    return pl.pallas_call(
        combine_body,
        in_specs=[IN_VMEM] * NX,
        out_specs=IN_VMEM,
        out_shape=jax.ShapeDtypeStruct((ROWS, GROUP * HEAD), BF),
        compiler_params=SMALL,
        cost_estimate=cost(1),
    )(*parts)


def local(tokens, w_query, key_matrix, value_matrix, w_output):
    c = lax.axis_index("ctx").astype(jnp.int32)
    h = lax.axis_index("head").astype(jnp.int32)
    where = jnp.stack([c // (NY * NX), (c // NX) % NY, c % NX])
    near = jnp.stack([h, h ^ 1])
    far = jnp.stack([h ^ 2, h ^ 3])
    width = tokens.shape[1]
    t_core = lax.ppermute(tokens, "head", swap(1))
    t_chip = lax.ppermute(tokens, "head", swap(2))
    slices = columns_apart(w_output, width)
    sums, rest, done = project_near(
        near, far, tokens, t_core, (w_query, key_matrix, value_matrix), [slices], 12
    )
    t_chip, done = lax.optimization_barrier((t_chip, done))
    t_far = lax.ppermute(t_chip, "head", swap(1))
    query = project_far(
        t_chip, t_far, rest[:1], sums[:1], [done], store_turned, (GROUP * HEAD, ROWS), 2
    )
    own = project_far(
        t_chip, t_far, rest[1:], sums[1:], [query], store_keys_values, (2 * ROWS, HEAD), 2
    )
    other = lax.ppermute(own, "ctx", shift(0, 1, 0))
    queries = [query] + [lax.ppermute(query, "ctx", shift(0, 0, -d)) for d in range(1, NX)]
    slices, _ = lax.optimization_barrier((slices, other))
    pieces = lax.all_to_all(slices, "head", 0, 0, tiled=True)
    level = pair_up(own, other, [queries[1], queries[3]])

    up = down = level
    state = None
    blocks = [(("own", 0), [own]), (("other", 0), [other])]
    for s in range(1, 5):
        up = lax.ppermute(up, "ctx", shift(1, 0, 0))
        if s < 4:
            down = lax.ppermute(down, "ctx", shift(-1, 0, 0))
        if s > 1:
            state = attend(where, queries, blocks, state, None, 6)
            up, down, state = lax.optimization_barrier((up, down, state))
            blocks = [(("both", s - 1), [last_up, last_down])]
        last_up, last_down = up, down
    blocks += [(("up", 4), [up])]
    sent = [None] * NX
    for group in ((2, 3), (1,), (0,)):
        parts = attend(where, queries, blocks, state, [group], 3 * len(group))
        for d, part in zip(group, parts):
            sent[d] = lax.ppermute(part, "ctx", shift(0, 0, d)) if d else part
    attended = combine(sent)
    a_chip = lax.ppermute(attended, "head", swap(2))
    a_core = lax.ppermute(attended, "head", swap(1))
    total, rest = products_near(near, far, [attended, a_core], pieces, 3)
    total, a_chip = lax.optimization_barrier((total, a_chip))
    a_far = lax.ppermute(a_chip, "head", swap(1))
    total = product(a_chip, rest[0], total, F32, 2)
    return product(a_far, rest[1], total, BF, 2)


def solution(mesh):
    return jax.shard_map(
        local,
        mesh=mesh,
        in_specs=(
            P("ctx", "head"),
            P(None, "head"),
            P(None, "head"),
            P(None, "head"),
            P("head", None),
        ),
        out_specs=P("ctx", "head"),
        check_vma=False,
    )
```

```python
import functools

import jax
import jax.numpy as jnp
from jax import lax
from jax.experimental import pallas as pl
from jax.experimental.pallas import tpu as pltpu
from jax.sharding import PartitionSpec as P

HEAD = 128
GROUP = 4
NZ, NY, NX = 8, 2, 4
ROWS = 256
WIDE = GROUP * ROWS
STAT_ROWS = 32
OUT_ROWS = GROUP * HEAD + STAT_ROWS
NEG = -1e30
C2 = HEAD**-0.5 * 1.4426950408889634
BF = jnp.bfloat16
F32 = jnp.float32
MIB = 1024 * 1024
SMALL = pltpu.CompilerParams(vmem_limit_bytes=16 * MIB)
LARGE = pltpu.CompilerParams(vmem_limit_bytes=40 * MIB)
IN_VMEM = pl.BlockSpec(memory_space=pltpu.VMEM)
IN_SMEM = pl.BlockSpec(memory_space=pltpu.SMEM)
IN_HBM = pl.BlockSpec(memory_space=pltpu.HBM)
ANYWHERE = pl.BlockSpec(memory_space=pl.ANY)


def place(z, y, x):
    return (z % NZ) * (NY * NX) + (y % NY) * NX + x % NX


def shift(dz, dy, dx):
    return [
        (place(z, y, x), place(z + dz, y + dy, x + dx))
        for z in range(NZ)
        for y in range(NY)
        for x in range(NX)
    ]


def swap(bit):
    return [(h, h ^ bit) for h in range(4)]


def cost(us):
    return pl.CostEstimate(
        flops=int(us * 10**9), bytes_accessed=int(us * 3 * 10**6), transcendentals=0
    )


def project_near(near, far, first, second, weights, after, us):
    depth = first.shape[1]
    count = len(weights)

    def rows(blocks_ref, step):
        return pl.ds(pl.multiple_of(blocks_ref[step] * depth, depth), depth)

    def body(near_ref, far_ref, first_ref, second_ref, *refs):
        w_refs, refs = refs[:count], refs[count + len(after) :]
        s_refs, f_refs, done_ref = refs[:count], refs[count : 2 * count], refs[-1]
        done_ref[...] = jnp.zeros(done_ref.shape, F32)
        for n in range(count):
            s_refs[n][...] = jnp.dot(
                first_ref[...], w_refs[n][rows(near_ref, 0), :], preferred_element_type=F32
            ) + jnp.dot(
                second_ref[...], w_refs[n][rows(near_ref, 1), :], preferred_element_type=F32
            )
            for step in range(2):
                f_refs[n][step] = w_refs[n][rows(far_ref, step), :]

    widths = [w.shape[1] for w in weights]
    out = pl.pallas_call(
        body,
        in_specs=[IN_SMEM] * 2 + [IN_VMEM] * (2 + count) + [ANYWHERE] * len(after),
        out_specs=[IN_VMEM] * (2 * count + 1),
        out_shape=[jax.ShapeDtypeStruct((first.shape[0], n), F32) for n in widths]
        + [jax.ShapeDtypeStruct((2, depth, n), BF) for n in widths]
        + [jax.ShapeDtypeStruct((8, HEAD), F32)],
        compiler_params=SMALL,
        cost_estimate=cost(us),
    )(near, far, first, second, *weights, *after)
    return out[:count], out[count : 2 * count], out[-1]


def project_far(first, second, weights, sums, after, finish, shape, us):
    count = len(weights)

    def body(first_ref, second_ref, *refs):
        w_refs, s_refs = refs[:count], refs[count : 2 * count]
        totals = []
        for n in range(count):
            total = s_refs[n][...] + jnp.dot(
                first_ref[...], w_refs[n][0], preferred_element_type=F32
            )
            totals.append(
                total + jnp.dot(second_ref[...], w_refs[n][1], preferred_element_type=F32)
            )
        finish(totals, refs[-1])

    return pl.pallas_call(
        body,
        in_specs=[IN_VMEM] * (2 + 2 * count) + [ANYWHERE] * len(after),
        out_specs=IN_VMEM,
        out_shape=jax.ShapeDtypeStruct(shape, BF),
        compiler_params=SMALL,
        cost_estimate=cost(us),
    )(first, second, *weights, *sums, *after)


def pair_up(own, other, after):
    def body(own_ref, other_ref, *refs):
        refs[-1][0] = own_ref[...]
        refs[-1][1] = other_ref[...]

    return pl.pallas_call(
        body,
        in_specs=[IN_VMEM] * 2 + [ANYWHERE] * len(after),
        out_specs=IN_VMEM,
        out_shape=jax.ShapeDtypeStruct((2,) + own.shape, own.dtype),
        compiler_params=SMALL,
        cost_estimate=cost(1),
    )(own, other, *after)


def columns_apart(w, width):
    count = w.shape[1] // width

    def body(w_ref, o_ref, sem):
        copies = [
            pltpu.make_async_copy(
                w_ref.at[:, pl.ds(n * width, width)], o_ref.at[n], sem.at[n]
            )
            for n in range(count)
        ]
        for c in copies:
            c.start()
        for c in copies:
            c.wait()

    return pl.pallas_call(
        body,
        in_specs=[IN_HBM],
        out_specs=IN_HBM,
        out_shape=jax.ShapeDtypeStruct((count, w.shape[0], width), w.dtype),
        scratch_shapes=[pltpu.SemaphoreType.DMA((count,))],
        compiler_params=SMALL,
        cost_estimate=cost(3),
    )(w)


def store_keys_values(totals, out):
    keys, values = totals
    turned = values.T.astype(BF)
    out[:ROWS] = keys.astype(BF)
    out[ROWS : ROWS + HEAD] = turned[:, :HEAD]
    out[ROWS + HEAD :] = turned[:, HEAD:]


def store_turned(totals, out):
    out[...] = totals[0].T.astype(BF)


def products_near(near, far, lefts, pieces, us):
    count = len(lefts)

    def body(near_ref, far_ref, pieces_ref, *refs):
        o_ref, rest_refs = refs[count], refs[count + 1 : count + 3]
        held, sem = refs[-2:]
        copies = [
            pltpu.make_async_copy(pieces_ref.at[near_ref[n]], held.at[n], sem.at[n])
            for n in range(count)
        ]
        copies += [
            pltpu.make_async_copy(pieces_ref.at[far_ref[n]], rest_refs[n], sem.at[count + n])
            for n in range(2)
        ]
        for c in copies:
            c.start()
        total = None
        for n in range(count):
            copies[n].wait()
            term = jnp.dot(refs[n][...], held[n], preferred_element_type=F32)
            total = term if total is None else total + term
        o_ref[...] = total
        for c in copies[count:]:
            c.wait()

    piece = jax.ShapeDtypeStruct(pieces.shape[1:], BF)
    total, *rest = pl.pallas_call(
        body,
        in_specs=[IN_SMEM] * 2 + [IN_HBM] + [IN_VMEM] * count,
        out_specs=[IN_VMEM] * 3,
        out_shape=[jax.ShapeDtypeStruct((lefts[0].shape[0], pieces.shape[2]), F32), piece, piece],
        scratch_shapes=[
            pltpu.VMEM((count,) + pieces.shape[1:], BF),
            pltpu.SemaphoreType.DMA((count + 2,)),
        ],
        compiler_params=SMALL,
        cost_estimate=cost(us),
    )(near, far, pieces, *lefts)
    return total, rest


def product(left, piece, total, out_type, us):
    def body(left_ref, piece_ref, total_ref, o_ref):
        term = jnp.dot(left_ref[...], piece_ref[...], preferred_element_type=F32)
        o_ref[...] = (total_ref[...] + term).astype(out_type)

    return pl.pallas_call(
        body,
        in_specs=[IN_VMEM] * 3,
        out_specs=IN_VMEM,
        out_shape=jax.ShapeDtypeStruct(total.shape, out_type),
        compiler_params=SMALL,
        cost_estimate=cost(us),
    )(left, piece, total)


def keys_of(ref):
    if len(ref.shape) == 2:
        return ref[:ROWS, :]
    return jnp.concatenate([ref[0, :ROWS, :], ref[1, :ROWS, :]], axis=0)


def values_of(ref):
    if len(ref.shape) == 2:
        return jnp.concatenate([ref[ROWS : ROWS + HEAD, :], ref[ROWS + HEAD :, :]], axis=1)
    return jnp.concatenate(
        [
            ref[0, ROWS : ROWS + HEAD, :],
            ref[0, ROWS + HEAD :, :],
            ref[1, ROWS : ROWS + HEAD, :],
            ref[1, ROWS + HEAD :, :],
        ],
        axis=1,
    )


def queries_of(q_refs, group):
    return jnp.concatenate(
        [q_refs[d][h * HEAD : (h + 1) * HEAD, :] for d in group for h in range(GROUP)], axis=1
    )


def fold(s):
    return jnp.sum(s.reshape(s.shape[0] // 8, 8, s.shape[1]), axis=0)


def attend_body(kinds, first, groups, where_ref, *refs):
    last = groups is not None
    groups = [(0, 1), (2, 3)] if groups is None else groups
    places = [d for group in groups for d in group]
    spans = [slice(group[0] * WIDE, (group[-1] + 1) * WIDE) for group in groups]
    q_refs, refs = refs[:NX], refs[NX:]
    many = sum(2 if name == "both" else 1 for name, _ in kinds)
    kv_refs, refs = list(refs[:many]), refs[many:]
    if not first:
        old, refs = refs[:3], refs[3:]
    if last:
        out_refs, refs = refs[: len(places)], refs[len(places) :]
    m_ref, l_ref, acc_ref = refs
    z, y, x = where_ref[0], where_ref[1], where_ref[2]
    if first:
        m_ref[...] = jnp.full(m_ref.shape, NEG, F32)
        l_ref[...] = jnp.zeros(l_ref.shape, F32)
        acc_ref[...] = jnp.zeros(acc_ref.shape, F32)
    else:
        for cols in spans:
            for new_ref, old_ref in zip((m_ref, l_ref, acc_ref), old):
                new_ref[:, cols] = old_ref[:, cols]

    def diagonal(d, ref):
        cols = slice(d * WIDE, (d + 1) * WIDE)

        def update():
            q = queries_of(q_refs, [d])
            s = jnp.dot(keys_of(ref), q, preferred_element_type=F32)
            if d == 0:
                key = lax.broadcasted_iota(jnp.int32, s.shape, 0)
                query = lax.broadcasted_iota(jnp.int32, s.shape, 1) % ROWS
                seen = key <= query
                s = jnp.where(seen, s, NEG)
            top = jnp.max(s, axis=0, keepdims=True)
            p = jnp.exp2((s - top) * C2)
            if d == 0:
                p = jnp.where(seen, p, 0.0)
            m_ref[:, cols] = top
            l_ref[:, cols] = fold(p)
            acc_ref[:, cols] = jnp.dot(values_of(ref), p.astype(BF), preferred_element_type=F32)

        if d == 0:
            update()
        else:
            pl.when(x + d < NX)(update)

    def whole(*blocks):
        keys = jnp.concatenate([keys_of(b) for b in blocks], axis=0)
        values = jnp.concatenate([values_of(b) for b in blocks], axis=1)
        for group, cols in zip(groups, spans):
            q = queries_of(q_refs, group)
            s = jnp.dot(keys, q, preferred_element_type=F32)
            m_old = m_ref[:, cols]
            m_new = jnp.maximum(m_old, jnp.max(s, axis=0, keepdims=True))
            p = jnp.exp2((s - m_new) * C2)
            total = fold(p)
            add = jnp.dot(values, p.astype(BF), preferred_element_type=F32)
            factor = jnp.exp2((m_old - m_new) * C2)
            m_ref[:, cols] = m_new
            l_ref[:, cols] = l_ref[:, cols] * factor + total
            acc_ref[:, cols] = acc_ref[:, cols] * factor + add

    for name, steps in kinds:
        ref = kv_refs.pop(0)
        if name == "own":
            for d in range(NX):
                diagonal(d, ref)
        elif name == "other":
            pl.when(y == 1)(functools.partial(whole, ref))
        elif name == "up":
            pl.when(z >= steps)(functools.partial(whole, ref))
        else:
            below = kv_refs.pop(0)
            pl.when(z >= NZ - steps)(functools.partial(whole, ref, below))
            pl.when((z >= steps) & (z < NZ - steps))(functools.partial(whole, ref))

    if last:
        for place_at, d in enumerate(places):
            out_ref = out_refs[place_at]
            tops, totals = [], []
            for h in range(GROUP):
                cols = slice((d * GROUP + h) * ROWS, (d * GROUP + h + 1) * ROWS)
                total = jnp.sum(l_ref[:, cols], axis=0, keepdims=True)
                scale = jnp.where(total > 0.0, 1.0 / total, 0.0)
                out_ref[h * HEAD : (h + 1) * HEAD, :] = (acc_ref[:, cols] * scale).astype(BF)
                tops.append(m_ref[:, cols])
                totals.append(total)
            flat = jnp.concatenate(tops + totals, axis=0)
            hi = flat.astype(BF).astype(F32)
            mid = (flat - hi).astype(BF).astype(F32)
            low = flat - hi - mid
            packed = jnp.concatenate([hi, mid, low, jnp.zeros_like(flat)], axis=0)
            out_ref[GROUP * HEAD :, :] = packed.astype(BF)


STATE = [(1, NX * WIDE), (8, NX * WIDE), (HEAD, NX * WIDE)]


def attend(where, queries, blocks, state, groups, us):
    kinds = [k for k, _ in blocks]
    first = state is None
    operands = [*queries, *[a for _, held in blocks for a in held]] + ([] if first else list(state))
    if groups is not None:
        shapes = [jax.ShapeDtypeStruct((OUT_ROWS, ROWS), BF)] * sum(map(len, groups))
        scratch = [pltpu.VMEM(s, F32) for s in STATE]
    else:
        shapes = [jax.ShapeDtypeStruct(s, F32) for s in STATE]
        scratch = []
    return pl.pallas_call(
        functools.partial(attend_body, kinds, first, groups),
        in_specs=[IN_SMEM] + [IN_VMEM] * len(operands),
        out_specs=[IN_VMEM] * len(shapes),
        out_shape=shapes,
        scratch_shapes=scratch,
        compiler_params=LARGE,
        cost_estimate=cost(us),
    )(where, *operands)


def combine_body(*refs):
    part_refs, out_ref = refs[:NX], refs[NX]
    tops, totals = [], []
    for ref in part_refs:
        packed = ref[GROUP * HEAD :, :].astype(F32)
        flat = packed[:8] + packed[8:16] + packed[16:24]
        tops.append(flat[:GROUP])
        totals.append(flat[GROUP:])
    best = functools.reduce(jnp.maximum, tops)
    weights = [t * jnp.exp2((m - best) * C2) for m, t in zip(tops, totals)]
    inverse = 1.0 / functools.reduce(jnp.add, weights)
    weights = [w * inverse for w in weights]
    for h in range(GROUP):
        rows = slice(h * HEAD, (h + 1) * HEAD)
        mixed = functools.reduce(
            jnp.add,
            [ref[rows, :].astype(F32) * w[h : h + 1] for ref, w in zip(part_refs, weights)],
        )
        out_ref[:, rows] = mixed.T.astype(BF)


def combine(parts):
    return pl.pallas_call(
        combine_body,
        in_specs=[IN_VMEM] * NX,
        out_specs=IN_VMEM,
        out_shape=jax.ShapeDtypeStruct((ROWS, GROUP * HEAD), BF),
        compiler_params=SMALL,
        cost_estimate=cost(1),
    )(*parts)


def local(tokens, w_query, key_matrix, value_matrix, w_output):
    c = lax.axis_index("ctx").astype(jnp.int32)
    h = lax.axis_index("head").astype(jnp.int32)
    where = jnp.stack([c // (NY * NX), (c // NX) % NY, c % NX])
    near = jnp.stack([h, h ^ 1])
    far = jnp.stack([h ^ 2, h ^ 3])
    width = tokens.shape[1]
    t_core = lax.ppermute(tokens, "head", swap(1))
    t_chip = lax.ppermute(tokens, "head", swap(2))
    slices = columns_apart(w_output, width)
    sums, rest, done = project_near(
        near, far, tokens, t_core, (w_query, key_matrix, value_matrix), [slices], 12
    )
    t_chip, done = lax.optimization_barrier((t_chip, done))
    t_far = lax.ppermute(t_chip, "head", swap(1))
    own = project_far(
        t_chip, t_far, rest[1:], sums[1:], [done], store_keys_values, (2 * ROWS, HEAD), 2
    )
    query = project_far(
        t_chip, t_far, rest[:1], sums[:1], [own], store_turned, (GROUP * HEAD, ROWS), 2
    )
    other = lax.ppermute(own, "ctx", shift(0, 1, 0))
    queries = [query] + [lax.ppermute(query, "ctx", shift(0, 0, -d)) for d in range(1, NX)]
    slices, _ = lax.optimization_barrier((slices, other))
    pieces = lax.all_to_all(slices, "head", 0, 0, tiled=True)
    level = pair_up(own, other, queries[3:])

    up = down = level
    state = None
    blocks = [(("own", 0), [own]), (("other", 0), [other])]
    for s in range(1, 5):
        up = lax.ppermute(up, "ctx", shift(1, 0, 0))
        if s < 4:
            down = lax.ppermute(down, "ctx", shift(-1, 0, 0))
        if s > 1:
            state = attend(where, queries, blocks, state, None, 6)
            up, down, state = lax.optimization_barrier((up, down, state))
            blocks = [(("both", s - 1), [last_up, last_down])]
        last_up, last_down = up, down
    blocks += [(("up", 4), [up])]
    sent = [None] * NX
    for group in ((2, 3), (1,), (0,)):
        parts = attend(where, queries, blocks, state, [group], 3 * len(group))
        for d, part in zip(group, parts):
            sent[d] = lax.ppermute(part, "ctx", shift(0, 0, d)) if d else part
    attended = combine(sent)
    a_chip = lax.ppermute(attended, "head", swap(2))
    a_core = lax.ppermute(attended, "head", swap(1))
    total, rest = products_near(near, far, [attended, a_core], pieces, 3)
    total, a_chip = lax.optimization_barrier((total, a_chip))
    a_far = lax.ppermute(a_chip, "head", swap(1))
    total = product(a_chip, rest[0], total, F32, 2)
    return product(a_far, rest[1], total, BF, 2)


def solution(mesh):
    return jax.shard_map(
        local,
        mesh=mesh,
        in_specs=(
            P("ctx", "head"),
            P(None, "head"),
            P(None, "head"),
            P(None, "head"),
            P("head", None),
        ),
        out_specs=P("ctx", "head"),
        check_vma=False,
    )
```
